768 devices in a mesh: panel: 6 (over z_lo), tile: 16 (over x, z_hi, core), lev: 8 (over y).
Axes of the slice: x: 4, y: 8, z: 12 (z_hi: 2, z_lo: 6; z = z_hi * 6 + z_lo), core: 2. Of those that a mesh axis runs over, the one named last changes fastest.
Arguments:
- parent: float32 [6, 8, 4, 512, 512], P('panel', 'lev', None, 'tile'), may hold values from -6 to 6
- courant: float32 [6, 8, 3, 512, 512], P('panel', 'lev', None, 'tile'), may hold values from 0.02 to 0.2
- edge_links: int32 [6, 4, 3], replicated, may hold values from 0 to 5, as said below
- nest_tracer: float32 [6, 64, 8, 4, 4096], P('panel', 'tile', 'lev'), may hold values from -6 to 6
- nest_weight: float32 [6, 64, 4096], P('panel', 'tile'), may hold values from 0.05 to 0.25
- nest_map: int32 [6, 64, 4096], P('panel', 'tile'), may hold values from 0 to 262143, as said below
- block_live: int32 [6, 64], P('panel', 'tile'), may hold values 0 or 1
Outputs:
- updated: float32 [6, 8, 4, 512, 512], P('panel', 'lev', None, 'tile')
The draws below stay inside these ranges and needn't reach their ends.
Inputs may be any that keep to these rules, and one draw needn't show every extreme that they name: `edge_links`: each side is paired with one other side, and the pairing is symmetric: if side s of panel p names (q, r, f), side r of panel q names (p, s, f). `nest_map`: nest cell (i, j) of a 64 x 64 block, at position i * 64 + j, maps to parent cell (a + i // 3) * 512 + b + j // 3 of the same panel for a corner (a, b) of that block; blocks may intersect.
All inputs are finite; a program needn't handle non-finite values. No bound on the sum of `block_live` on one device may be relied on, other than what follows from the above.
Results may differ from the reference program's by a relative error of at most 0.00002.
Values sent between devices are 32-bit elements; how exact they have to be, the bound alone decides.
No kernel may reach another device: no remote copies, remote signals or barrier semaphores. Data moves between devices by JAX's collectives and lax.ppermute only.
A program may use at most 64 MiB of HBM per device.

```python
import math
import jax
import jax.numpy as jnp
import numpy as np

TRACERS = 4
BEDGE = 64
BLOCK = 4096
WIN = 22
SIDE = 512
LEVELS = 8
PANELS = 6
NEST_BLOCKS = 64


def draw_edge_links(key, part):
    key = jax.random.fold_in(key, 11)
    order_key, flip_key = jax.random.split(key)
    half_count = PANELS // 2
    first_list = [4 * p for p in range(half_count)]
    second_list = [4 * (p + half_count) + 1 for p in range(half_count)]
    taken = set(first_list) | set(second_list)
    remaining = np.array([s for s in range(4 * PANELS) if s not in taken], dtype=np.int32)
    fixed_first = np.array(first_list, dtype=np.int32)
    fixed_second = np.array(second_list, dtype=np.int32)
    order = jax.random.permutation(order_key, jnp.asarray(remaining))
    firsts = jnp.concatenate([jnp.asarray(fixed_first), order[0::2]])
    seconds = jnp.concatenate([jnp.asarray(fixed_second), order[1::2]])
    flips = jax.random.randint(flip_key, (2 * PANELS,), 0, 2, dtype=jnp.int32)
    table = jnp.zeros((4 * PANELS, 3), jnp.int32)
    table = table.at[firsts].set(jnp.stack([seconds // 4, seconds % 4, flips], 1))
    table = table.at[seconds].set(jnp.stack([firsts // 4, firsts % 4, flips], 1))
    return table.reshape(PANELS, 4, 3)


def draw_nest_map(key, part):
    key = jax.random.fold_in(key, 23)
    row_key, col_key, high_key, low_key = jax.random.split(key, 4)
    span_count = SIDE - WIN + 1
    anchor_rows = jax.random.randint(row_key, (PANELS, NEST_BLOCKS), 0, span_count, dtype=jnp.int32)
    anchor_cols = jax.random.randint(col_key, (PANELS, NEST_BLOCKS), 0, span_count, dtype=jnp.int32)
    high_slot = jax.random.randint(high_key, (PANELS, 1), 0, NEST_BLOCKS, dtype=jnp.int32)
    low_slot = (high_slot + jax.random.randint(low_key, (PANELS, 1), 1, NEST_BLOCKS, dtype=jnp.int32)) % NEST_BLOCKS
    slots = jnp.arange(NEST_BLOCKS, dtype=jnp.int32)[None, :]
    anchor_rows = jnp.where(slots == high_slot, span_count - 1, jnp.where(slots == low_slot, 0, anchor_rows))
    anchor_cols = jnp.where(slots == high_slot, span_count - 1, jnp.where(slots == low_slot, 0, anchor_cols))
    position = jnp.arange(BLOCK, dtype=jnp.int32)
    offset_rows = position // BEDGE // 3
    offset_cols = position % BEDGE // 3
    return (anchor_rows[..., None] + offset_rows) * SIDE + anchor_cols[..., None] + offset_cols


def with_ends(entries, own_key, smallest, top_value):
    longest = entries.shape.index(max(entries.shape))
    spots = []
    for shift in (0, 1):
        where = [jax.random.randint(jax.random.fold_in(own_key, axis), (), 0, length) for axis, length in enumerate(entries.shape)]
        where[longest] = (where[longest] + shift) % entries.shape[longest]
        spots.append(tuple(where))
    return entries.at[spots[0]].set(smallest).at[spots[1]].set(top_value)


def level_of(rng, extent, pieces, least, top_value):
    def one(dim, shards_of):
        heights = jax.random.uniform(jax.random.fold_in(jax.random.fold_in(rng, 6), dim), (shards_of,), jnp.float32, least / len(pieces), top_value / len(pieces))
        return jnp.repeat(jnp.exp(heights), extent[dim] // shards_of).reshape((-1,) + (1,) * (len(extent) - dim - 1))

    loudness = one(*pieces[0])
    for cut in pieces[1:]:
        loudness = loudness * one(*cut)
    return loudness


def noise(own_key, extent, deviation, most, cuts=(), kind=jnp.bfloat16):
    entries = jax.random.normal(own_key, extent, jnp.float32) * deviation
    if len(cuts) > 0:
        entries = level_of(own_key, extent, cuts, -0.22, 0.18) * entries
    return jnp.clip(entries, min=-most, max=most).astype(kind)


def setup_inputs(seed: int = 0) -> dict:
    seeds = jax.random.split(jax.random.key(seed), 8)
    parent = noise(seeds[0], (PANELS, LEVELS, TRACERS, SIDE, SIDE), 1.0, 6.0, ((0, 6), (1, 8), (3, 16)), jnp.float32)
    courant = jnp.clip(0.02 + 0.18 * jax.random.uniform(seeds[1], (PANELS, LEVELS, 3, SIDE, SIDE), jnp.float32) ** level_of(seeds[1], (PANELS, LEVELS, 3, SIDE, SIDE), ((0, 6), (1, 8), (3, 16)), -0.2, 0.2), 0.02, 0.2)
    edge_links = draw_edge_links(jax.random.fold_in(seeds[7], 71), 0)
    nest_tracer = noise(seeds[3], (PANELS, NEST_BLOCKS, LEVELS, TRACERS, BLOCK), 1.0, 6.0, ((0, 6), (1, 16), (2, 8)), jnp.float32)
    nest_weight = jnp.clip(jnp.exp(math.log(0.25) - 1.609438 * jax.random.uniform(seeds[4], (PANELS, NEST_BLOCKS, BLOCK), jnp.float32) ** level_of(seeds[4], (PANELS, NEST_BLOCKS, BLOCK), ((0, 6), (1, 16)), -0.2, 0.2)), 0.05, 0.25)
    nest_map = draw_nest_map(jax.random.fold_in(seeds[7], 71), 0)
    block_live = with_ends((jax.random.randint(seeds[6], (PANELS, NEST_BLOCKS), 0, 4) < 3).astype(jnp.int32), jax.random.fold_in(seeds[6], 1), 0, 1)
    return {"parent": parent, "courant": courant, "edge_links": edge_links, "nest_tracer": nest_tracer, "nest_weight": nest_weight, "nest_map": nest_map, "block_live": block_live}


def panel_borders(field_now):
    side_count = field_now.shape[-1]
    return jnp.stack([field_now[..., :, 0], field_now[..., :, side_count - 1], field_now[..., 0, :], field_now[..., side_count - 1, :]], 0)


def transport(field_now, coefficients, padded):
    west_cells = padded[..., 1:-1, :-2]
    east_cells = padded[..., 1:-1, 2:]
    north_cells = padded[..., :-2, 1:-1]
    south_cells = padded[..., 2:, 1:-1]
    speed_x = coefficients[:, 0][:, None]
    speed_y = coefficients[:, 1][:, None]
    mixing = coefficients[:, 2][:, None]
    return field_now - speed_x * (field_now - west_cells) - speed_y * (field_now - north_cells) + mixing * (west_cells + east_cells + north_cells + south_cells - 4.0 * field_now)


def reference(parent, courant, edge_links, nest_tracer, nest_weight, nest_map, block_live):
    borders = jnp.stack([panel_borders(parent[panel_index]) for panel_index in range(PANELS)], 0)
    results = []
    for panel_index in range(PANELS):
        field_now = parent[panel_index]
        halos = []
        for border in range(4):
            partner = edge_links[panel_index, border]
            strip_line = borders[partner[0], partner[1]]
            strip_line = jnp.where(partner[2] == 1, jnp.flip(strip_line, -1), strip_line)
            halos.append(strip_line)
        padded = jnp.pad(field_now, ((0, 0), (0, 0), (1, 1), (1, 1)))
        padded = padded.at[:, :, 1:-1, 0].set(halos[0])
        padded = padded.at[:, :, 1:-1, -1].set(halos[1])
        padded = padded.at[:, :, 0, 1:-1].set(halos[2])
        padded = padded.at[:, :, -1, 1:-1].set(halos[3])
        moved_field = transport(field_now, courant[panel_index], padded)
        weights = nest_weight[panel_index] * block_live[panel_index][:, None].astype(jnp.float32)
        cell_index = nest_map[panel_index].reshape(-1)
        values = nest_tracer[panel_index] * weights[:, None, None, :]
        values = jnp.moveaxis(values, 0, 2).reshape(LEVELS, TRACERS, -1)
        mass_sum = jnp.zeros((LEVELS, TRACERS, SIDE * SIDE), jnp.float32).at[:, :, cell_index].add(values)
        cover_sum = jnp.zeros((SIDE * SIDE,), jnp.float32).at[cell_index].add(weights.reshape(-1))
        blended = (moved_field + mass_sum.reshape(LEVELS, TRACERS, SIDE, SIDE)) / (1.0 + cover_sum.reshape(SIDE, SIDE))
        results.append(blended)
    return jnp.stack(results, 0)
```

```python
import functools

import jax
import jax.numpy as jnp
from jax import lax
from jax.experimental import pallas as pl
from jax.experimental.pallas import tpu as pltpu
from jax.sharding import PartitionSpec as P

WIN = 22
WROWS = 24
FAR = -(64 * 512)
ZROW = 4 * WROWS
ZMETA = ZROW + 16
ZALL = ZMETA + 8
GROWS = 2 * ZROW
GLINES = GROWS + 32
GMETA = GLINES + 64
GALL = GMETA + 8
VMEM = pl.BlockSpec(memory_space=pltpu.VMEM)
SMEM = pl.BlockSpec(memory_space=pltpu.SMEM)


def tile_of(x, z, c):
    return (x * 2 + z) * 2 + c


def place_of():
    t = lax.axis_index("tile")
    return t, t // 4, (t // 2) % 2, t % 2


def lane_rows(line):
    return jnp.concatenate([line[:, 128 * k : 128 * (k + 1)] for k in range(4)], 0)


def three(x):
    hi = x.astype(jnp.bfloat16)
    rest = x - hi.astype(jnp.float32)
    mid = rest.astype(jnp.bfloat16)
    low = (rest - mid.astype(jnp.float32)).astype(jnp.bfloat16)
    return hi, mid, low


def dot(a, b):
    return jnp.dot(a, b, preferred_element_type=jnp.float32)


def border_kernel(parent_ref, slot_ref, rows_ref):
    t, _, _, c = place_of()
    west = parent_ref[:, :, 0:128].reshape(128, 128).T[0:1]
    east = parent_ref[:, :, 384:512].reshape(128, 128).T[127:128]
    first = lane_rows(parent_ref[:, 0, :])
    last = lane_rows(parent_ref[:, 31, :])
    line = jnp.where(t == 0, first, last)
    packet = jnp.concatenate([west, east, jnp.zeros((6, 128), jnp.float32), line], 0)
    for k in range(12):
        slot_ref[k] = packet
    rows_ref[0:16] = jnp.where(c == 0, first, last)
    rows_ref[16:32] = jnp.where(c == 0, last, first)


def pool_kernel(x_ref, w_ref, map_ref, live_ref, rows_ref, out_ref):
    pieces = []
    for blk in range(4):
        live = live_ref[0, blk].astype(jnp.float32)
        weight = w_ref[pl.ds(blk, 32, stride=4), :] * live
        for m in range(4):
            pieces.append(x_ref[blk, pl.ds(m, 32, stride=4), :] * weight)
        pieces.append(weight)
    parts = jnp.concatenate(three(jnp.concatenate(pieces, 1)), 0)
    row = lax.broadcasted_iota(jnp.int32, (48, 96), 0)
    col = lax.broadcasted_iota(jnp.int32, (48, 96), 1)
    odd = (row >= WROWS).astype(jnp.int32)
    nest_row = 2 * (col & 31) + odd
    take = ((nest_row * 43) >> 7) == row - WROWS * odd
    halves = dot(take.astype(jnp.float32).astype(jnp.bfloat16), parts)
    lane = lax.broadcasted_iota(jnp.int32, (WROWS, halves.shape[1]), 1)
    pooled = jnp.where((lane & 64) == 0, halves[:WROWS], halves[WROWS:])
    pooled = jnp.concatenate([pooled[:, 640 * b : 640 * (b + 1)] for b in range(4)], 0)
    row = lax.broadcasted_iota(jnp.int32, (640, 128), 0)
    col = lax.broadcasted_iota(jnp.int32, (640, 128), 1)
    into = (row >> 7) * WIN + (((row & 63) * 43) >> 7)
    gather = (into == col).astype(jnp.float32).astype(jnp.bfloat16)
    hi, mid, low = three(pooled)
    out_ref[0:ZROW] = dot(hi, gather) + dot(mid, gather) + dot(low, gather)
    out_ref[ZROW:ZMETA] = rows_ref[0:16]
    lane = lax.broadcasted_iota(jnp.int32, (8, 128), 1)
    meta = jnp.full((8, 128), FAR, jnp.int32)
    for blk in range(4):
        corner = jnp.where(live_ref[0, blk] != 0, map_ref[blk : blk + 1, 0:1], FAR)
        meta = jnp.where(lane == blk, corner, meta)
    out_ref[ZMETA:ZALL] = meta.astype(jnp.float32)


def pack_kernel(own_ref, other_ref, slots_ref, rows_ref, links_ref, out_ref):
    _, x, _, c = place_of()
    panel = lax.axis_index("panel")
    out_ref[0:ZROW] = own_ref[0:ZROW]
    out_ref[ZROW:GROWS] = other_ref[0:ZROW]
    out_ref[GROWS : GROWS + 16] = rows_ref[16:32]
    out_ref[GROWS + 16 : GLINES] = other_ref[ZROW:ZMETA]
    lane = lax.broadcasted_iota(jnp.int32, (4, 128), 1)
    trc = lax.broadcasted_iota(jnp.int32, (4, 128), 0)
    part = lax.broadcasted_iota(jnp.int32, (16, 128), 0) >> 2
    for side in range(4):
        q = links_ref[panel, side, 0]
        r = links_ref[panel, side, 1]
        piece = jnp.zeros((4, 128), jnp.float32)
        for z in range(2):
            column = slots_ref[2 * q + z, pl.ds(r & 1, 1), :]
            start = 64 * z + 32 * c
            for m in range(4):
                turned = pltpu.roll(jnp.broadcast_to(column, (8, 128)), (start - 32 * m + 128) % 128, 1)[0:4]
                inside = (trc == m) & (lane >= start) & (lane < start + 32)
                piece = jnp.where(inside, turned, piece)
        column_lines = jnp.where(part == x, jnp.concatenate([piece] * 4, 0), 0.0)
        row_line = slots_ref[2 * q + (r & 1), 8:24, :]
        holds = ((r == 2) & (x == 0) & (c == 0)) | ((r == 3) & (x == 3) & (c == 1))
        row_lines = jnp.where(holds, row_line, 0.0)
        out_ref[GLINES + 16 * side : GLINES + 16 * (side + 1)] = jnp.where(r < 2, column_lines, row_lines)
    lane = lax.broadcasted_iota(jnp.int32, (8, 128), 1)
    out_ref[GMETA:GALL] = jnp.where(
        lane < 4, own_ref[ZMETA:ZALL], pltpu.roll(other_ref[ZMETA:ZALL], 4, 1)
    )


def final_kernel(near_ref, far_ref, parent_ref, courant_ref, links_ref, out_ref, total_ref, lines_ref, meta_ref, corner_ref, sem):
    t, x, z, c = place_of()
    panel = lax.axis_index("panel")
    refs = (near_ref, far_ref)
    for k in range(2):
        for s in range(4):
            meta_ref[4 * k + s : 4 * k + s + 1] = refs[k][s, GMETA : GMETA + 1]
    copy = pltpu.make_async_copy(meta_ref, corner_ref, sem)
    copy.start()
    total_ref[:, 16:56, :] = jnp.zeros((5, 40, 640), jnp.float32)

    lines = near_ref[0, GLINES:GMETA]
    for s in range(1, 4):
        lines = lines + near_ref[s, GLINES:GMETA]
    for s in range(4):
        lines = lines + far_ref[s, GLINES:GMETA]
    row = lax.broadcasted_iota(jnp.int32, (128, 128), 0)
    col = lax.broadcasted_iota(jnp.int32, (128, 128), 1)
    mirror = (row + col == 127).astype(jnp.float32).astype(jnp.bfloat16)
    hi, mid, low = three(lines)
    turned = dot(hi, mirror) + dot(mid, mirror) + dot(low, mirror)
    for side in range(4):
        for k in range(4):
            lines_ref[0, side, 4 * k : 4 * k + 4] = lines[16 * side + 4 * k : 16 * side + 4 * k + 4]
            back = 3 - k
            lines_ref[1, side, 4 * k : 4 * k + 4] = turned[16 * side + 4 * back : 16 * side + 4 * back + 4]

    def column_halo(side):
        flip = links_ref[panel, side, 2]
        piece = lines_ref[flip, side, pl.ds(4 * x, 4), :]
        piece = jnp.concatenate([piece, piece], 0)
        piece = pltpu.roll(piece, (128 - 32 * (t % 4)) % 128, 1)
        piece = jnp.concatenate([piece, jnp.zeros((120, 128), jnp.float32)], 0)
        return piece.T[0:32]

    west_halo = column_halo(0)
    east_halo = column_halo(1)
    north_line = lines_ref[links_ref[panel, 2, 2], 2]
    south_line = lines_ref[links_ref[panel, 3, 2], 3]
    kept = slice(GROWS, GROWS + 16)
    passed = slice(GROWS + 16, GLINES)
    before = near_ref if False else far_ref
    north_of_0 = far_ref[lax.rem(x + 3 + z, 4), passed, :]
    north_of_1 = far_ref[x, kept, :]
    north = jnp.where(c == 0, north_of_0, north_of_1)
    south_of_0 = far_ref[x, kept, :]
    south_of_1 = far_ref[lax.rem(x + z, 4), passed, :]
    south = jnp.where(c == 0, south_of_0, south_of_1)
    north = jnp.where(t == 0, north_line, north)
    south = jnp.where(t == 15, south_line, south)

    copy.wait()
    lane = lax.broadcasted_iota(jnp.int32, (32, 128), 1)
    sub = lax.broadcasted_iota(jnp.int32, (32, 128), 0)
    first_row = 32 * t
    for k in range(2):

        def deposit(i, carry, k=k):
            s = i // 8
            j = lax.rem(i, 8)
            corner = corner_ref[4 * k + s, j].astype(jnp.int32)
            r = (corner >> 9) - first_row

            @pl.when((r > -(WIN + 1)) & (r < 32))
            def _():
                b = corner & 511
                start = pl.multiple_of(j * WROWS, 8)
                window = refs[k][s, pl.ds(start, WROWS), :]
                window = jnp.concatenate([window, jnp.zeros((8, 128), jnp.float32)], 0)
                at = r + 24
                rows = pl.ds(pl.multiple_of((at >> 3) * 8, 8), 32)
                window = pltpu.roll(window, at & 7, 0)
                q = pl.multiple_of((b >> 7) * 128, 128)
                off = b & 127
                low_side = (lane >= off) & (lane < off + WIN)
                high_side = lane < off + WIN - 128
                for m in range(5):
                    moved = pltpu.roll(window, (off - WIN * m + 128) % 128, 1)
                    here = pl.ds(q, 128)
                    total_ref[m, rows, here] += jnp.where(low_side, moved, 0.0)
                    there = pl.ds(pl.multiple_of(q + 128, 128), 128)
                    total_ref[m, rows, there] += jnp.where(high_side, moved, 0.0)

            return carry

        lax.fori_loop(0, 32, deposit, 0)

    def deposited(m):
        mass = total_ref[m, 24:56, 0:512]
        spill = total_ref[m, 16:56, 512:640]
        spill = pltpu.roll(spill, 33, 0)[0:32]
        return jnp.concatenate([mass[:, 0:128] + spill, mass[:, 128:512]], 1)

    scale = 1.0 / (1.0 + deposited(4))
    u = courant_ref[0]
    v = courant_ref[1]
    mix = courant_ref[2]
    column = lax.broadcasted_iota(jnp.int32, (32, 512), 1)
    line = lax.broadcasted_iota(jnp.int32, (32, 512), 0)
    for m in range(4):
        here = parent_ref[m]
        west = jnp.where(column == 0, west_halo[:, m : m + 1], pltpu.roll(here, 1, 1))
        east = jnp.where(column == 511, east_halo[:, m : m + 1], pltpu.roll(here, 511, 1))
        north_row = jnp.concatenate([north[4 * k + m : 4 * k + m + 1] for k in range(4)], 1)
        south_row = jnp.concatenate([south[4 * k + m : 4 * k + m + 1] for k in range(4)], 1)
        up = jnp.where(line == 0, north_row, pltpu.roll(here, 1, 0))
        down = jnp.where(line == 31, south_row, pltpu.roll(here, 31, 0))
        moved = here - u * (here - west) - v * (here - up) + mix * (west + east + up + down - 4.0 * here)
        out_ref[m] = (moved + deposited(m)) * scale


def shape(*dims):
    return jax.ShapeDtypeStruct(dims, jnp.float32)


def body(parent, courant, edge_links, nest_tracer, nest_weight, nest_map, block_live):
    params = pltpu.CompilerParams(vmem_limit_bytes=32 * 1024 * 1024)
    parent = parent[0, 0]
    slots, rows = pl.pallas_call(
        border_kernel,
        out_shape=(shape(12, 24, 128), shape(32, 128)),
        in_specs=[VMEM],
        out_specs=(VMEM, VMEM),
        compiler_params=params,
    )(parent)
    lines_of_z = [
        [p * 16 + tile_of(x, z, c) for p in range(6) for z in range(2)] for x in range(4) for c in range(2)
    ]
    slots = lax.all_to_all(slots, ("panel", "tile"), 0, 0, tiled=True, axis_index_groups=lines_of_z)

    values = nest_tracer[0, :, 0].reshape(4, 4, 32, 128).transpose(0, 2, 1, 3).reshape(4, 128, 128)
    weights = nest_weight[0].reshape(4, 32, 128).transpose(1, 0, 2).reshape(128, 128)
    own = pl.pallas_call(
        pool_kernel,
        grid=(1,),
        out_shape=shape(ZALL, 128),
        in_specs=[
            VMEM,
            VMEM,
            pl.BlockSpec((4, 128), lambda i: (0, 0)),
            SMEM,
            VMEM,
        ],
        out_specs=VMEM,
        compiler_params=params,
    )(values, weights, nest_map[0], block_live, rows)
    other = lax.ppermute(own, "tile", [(t, t ^ 2) for t in range(16)])
    packed = pl.pallas_call(
        pack_kernel,
        out_shape=shape(GALL, 128),
        in_specs=[VMEM, VMEM, VMEM, VMEM, SMEM],
        out_specs=VMEM,
        compiler_params=params,
    )(own, other, slots, rows, edge_links)
    chips = [[tile_of(x, z, c) for x in range(4)] for z in range(2) for c in range(2)]
    near = lax.all_gather(packed, "tile", axis=0, axis_index_groups=chips)
    far = lax.ppermute(near, "tile", [(t, t ^ 1) for t in range(16)])
    out = pl.pallas_call(
        final_kernel,
        out_shape=shape(4, 32, 512),
        in_specs=[VMEM, VMEM, VMEM, VMEM, SMEM],
        out_specs=VMEM,
        scratch_shapes=[
            pltpu.VMEM((5, 88, 640), jnp.float32),
            pltpu.VMEM((2, 4, 16, 128), jnp.float32),
            pltpu.VMEM((8, 128), jnp.float32),
            pltpu.SMEM((8, 128), jnp.float32),
            pltpu.SemaphoreType.DMA,
        ],
        compiler_params=params,
    )(near, far, parent, courant[0, 0], edge_links)
    return out[None, None]


def solution(mesh):
    placed = (
        P("panel", "lev", None, "tile", None),
        P("panel", "lev", None, "tile", None),
        P(),
        P("panel", "tile", "lev", None, None),
        P("panel", "tile", None),
        P("panel", "tile", None),
        P("panel", "tile"),
    )
    return jax.shard_map(
        body,
        mesh=mesh,
        in_specs=placed,
        out_specs=P("panel", "lev", None, "tile", None),
        check_vma=False,
    )
```

```python
import jax
import jax.numpy as jnp
from jax import lax
from jax.experimental import pallas as pl
from jax.experimental.pallas import tpu as pltpu
from jax.sharding import PartitionSpec as P

WIN = 22
WROWS = 24
FAR = -(64 * 512)
OWN = 4 * WROWS
ZALL = OWN + 8
BOTH = 2 * OWN
SIDES = BOTH
KEPT = SIDES + 8
PASSED = KEPT + 16
SLOT = PASSED + 16
META = 112
VMEM = pl.BlockSpec(memory_space=pltpu.VMEM)
SMEM = pl.BlockSpec(memory_space=pltpu.SMEM)
ANY = pl.BlockSpec(memory_space=pl.ANY)


def tile_of(x, z, c):
    return (x * 2 + z) * 2 + c


def place_of():
    t = lax.axis_index("tile")
    return t, t // 4, (t // 2) % 2, t % 2


def lane_rows(line):
    return jnp.concatenate([line[:, 128 * k : 128 * (k + 1)] for k in range(4)], 0)


def three(x):
    hi = x.astype(jnp.bfloat16)
    rest = x - hi.astype(jnp.float32)
    mid = rest.astype(jnp.bfloat16)
    low = (rest - mid.astype(jnp.float32)).astype(jnp.bfloat16)
    return hi, mid, low


def dot(a, b):
    return jnp.dot(a, b, preferred_element_type=jnp.float32)


def dot_exact(a, picks):
    hi, mid, low = three(a)
    return dot(hi, picks) + dot(mid, picks) + dot(low, picks)


def picks_of(mask):
    return mask.astype(jnp.float32).astype(jnp.bfloat16)


def iota(dims, axis):
    return lax.broadcasted_iota(jnp.int32, dims, axis)


def pool_kernel(
    x_hbm, w_hbm, map_hbm, parent_hbm, live_hbm, out_ref, packet_ref, x_ref, w_ref, map_ref, live_ref, west_ref, east_ref, ends_ref, sems
):
    t, _, _, c = place_of()
    copies = [
        pltpu.make_async_copy(live_hbm, live_ref, sems.at[0]),
        pltpu.make_async_copy(w_hbm, w_ref, sems.at[1]),
        pltpu.make_async_copy(x_hbm, x_ref, sems.at[2]),
        pltpu.make_async_copy(map_hbm.at[:, 0:128], map_ref, sems.at[3]),
        pltpu.make_async_copy(parent_hbm.at[:, :, 0:128], west_ref, sems.at[4]),
        pltpu.make_async_copy(parent_hbm.at[:, :, 384:512], east_ref, sems.at[5]),
        pltpu.make_async_copy(parent_hbm.at[:, 0:8, :], ends_ref.at[0], sems.at[6]),
        pltpu.make_async_copy(parent_hbm.at[:, 24:32, :], ends_ref.at[1], sems.at[7]),
    ]
    for copy in copies:
        copy.start()
    row = iota((48, 96), 0)
    col = iota((48, 96), 1)
    odd = (row >= WROWS).astype(jnp.int32)
    nest_row = 2 * (col & 31) + odd
    take = picks_of(((nest_row * 43) >> 7) == row - WROWS * odd)
    row = iota((640, 128), 0)
    col = iota((640, 128), 1)
    gather = picks_of((row >> 7) * WIN + (((row & 63) * 43) >> 7) == col)
    for copy in copies[0:3]:
        copy.wait()
    pieces = []
    for blk in range(4):
        live = live_ref[0, blk].astype(jnp.float32)
        weight = w_ref[pl.ds(blk, 32, stride=4), :] * live
        for m in range(4):
            pieces.append(x_ref[blk, pl.ds(m, 32, stride=4), :] * weight)
        pieces.append(weight)
    parts = jnp.concatenate(three(jnp.concatenate(pieces, 1)), 0)
    halves = dot(take, parts)
    lane = iota((WROWS, halves.shape[1]), 1)
    pooled = jnp.where((lane & 64) == 0, halves[:WROWS], halves[WROWS:])
    pooled = jnp.concatenate([pooled[:, 640 * b : 640 * (b + 1)] for b in range(4)], 0)
    out_ref[0:OWN] = dot_exact(pooled, gather)
    for copy in copies[3:8]:
        copy.wait()
    lane = iota((1, 128), 1)
    meta = jnp.zeros((1, 128), jnp.int32)
    for blk in range(4):
        corner = jnp.where(live_ref[0, blk] != 0, map_ref[blk : blk + 1, 0:1], FAR)
        meta = jnp.where(lane == META + blk, corner, meta)
    out_ref[0:1] = jnp.where(lane < META, out_ref[0:1], meta.astype(jnp.float32))
    first = lane_rows(ends_ref[0, :, 0, :])
    last = lane_rows(ends_ref[1, :, 7, :])
    edge = jnp.where(c == 0, first, last)
    for b in range(4):
        out_ref[WROWS * b + WIN : WROWS * (b + 1)] = edge[2 * b : 2 * b + 2]
    out_ref[OWN:ZALL] = edge[8:16]
    west = west_ref[...].reshape(128, 128).T[0:1]
    east = east_ref[...].reshape(128, 128).T[127:128]
    line = jnp.where(t == 0, first, last)
    packet_ref[0:24] = jnp.concatenate([west, east, jnp.zeros((6, 128), jnp.float32), line], 0)
    packet_ref[24:40] = jnp.where(c == 0, last, first)


def border_kernel(packet_ref, slot_ref):
    for k in range(12):
        slot_ref[k] = packet_ref[0:24]


def inner_kernel(parent_ref, courant_ref, after_ref, out_ref):
    u = courant_ref[0]
    v = courant_ref[1]
    mix = courant_ref[2]
    column = iota((32, 512), 1)
    line = iota((32, 512), 0)
    for m in range(4):
        here = parent_ref[m]
        west = jnp.where(column == 0, 0.0, pltpu.roll(here, 1, 1))
        east = jnp.where(column == 511, 0.0, pltpu.roll(here, 511, 1))
        up = jnp.where(line == 0, 0.0, pltpu.roll(here, 1, 0))
        down = jnp.where(line == 31, 0.0, pltpu.roll(here, 31, 0))
        out_ref[m] = here - u * (here - west) - v * (here - up) + mix * (west + east + up + down - 4.0 * here)


def pack_kernel(own_ref, other_ref, slots_ref, links_ref, packet_ref, after_ref, out_ref):
    _, x, z, c = place_of()
    panel = lax.axis_index("panel")
    for s in range(4):
        out_ref[s, 0:OWN] = own_ref[0:OWN]
        out_ref[s, OWN:BOTH] = other_ref[0:OWN]
    passed = jnp.concatenate(
        [other_ref[WROWS * b + WIN : WROWS * (b + 1)] for b in range(4)] + [other_ref[OWN:ZALL]], 0
    )

    sides = (0, 1, 2 + z)
    links = [(links_ref[panel, s, 0], links_ref[panel, s, 1], links_ref[panel, s, 2]) for s in sides]
    halves = [(0, z ^ links[0][2]), (1, z ^ links[1][2]), (2, 0), (2, 1)]
    columns = []
    for k, half in halves:
        q, r, _ = links[k]
        columns.append(slots_ref[2 * q + half, pl.ds(r & 1, 1), :])
    columns = jnp.concatenate(columns + [jnp.zeros((4, 128), jnp.float32)], 0)
    near = iota((128, 128), 0)
    far = iota((128, 128), 1)
    back = dot_exact(columns, picks_of((near ^ 31) == far))
    columns = [jnp.where(links[k][2] == 1, back[i : i + 1], columns[i : i + 1]) for i, (k, _) in enumerate(halves)]
    lines = jnp.concatenate([slots_ref[2 * q + (r & 1), 8:24, :] for q, r, _ in links], 0)
    back = dot_exact(lines, picks_of((near ^ 127) == far))
    lines = [
        jnp.where(
            links[k][2] == 1,
            jnp.concatenate([back[16 * k + 4 * (3 - p) : 16 * k + 4 * (4 - p)] for p in range(4)], 0),
            lines[16 * k : 16 * (k + 1)],
        )
        for k in range(3)
    ]
    holds = [((r == 2) & (x == 0) & (c == 0)) | ((r == 3) & (x == 3) & (c == 1)) for _, r, _ in links]

    lane = iota((16, 128), 1)
    trc = iota((16, 128), 0) & 3
    part = iota((16, 128), 0) >> 2

    def spread(a):
        return a + pltpu.roll(a, 32, 1) + pltpu.roll(a, 64, 1) + pltpu.roll(a, 96, 1)

    for k in range(2):
        q, r, f = links[k]
        to_chip = jnp.where(f == 1, 3 - x, x)
        to_core = jnp.where(f == 1, 1 - c, c)
        for core in range(2):
            group = 2 * z + core
            cut = jnp.where((lane >> 5) == group, lines[k], 0.0)
            cut = jnp.where((lane >> 5) == trc, spread(cut), 0.0)
            cut = cut + pltpu.roll(cut, 15, 0) + pltpu.roll(cut, 14, 0) + pltpu.roll(cut, 13, 0)
            for s in range(4):
                from_column = jnp.where((to_chip == s) & (to_core == core), columns[k], 0.0)
                from_line = jnp.where(holds[k], cut[4 * s : 4 * s + 1], 0.0)
                at = SIDES + 2 * k + core
                out_ref[s, at : at + 1] = jnp.where(r < 2, from_column, from_line)

    q, r, f = links[2]
    to_chip = jnp.where(f == 1, 3 - x, x)
    ends = jnp.zeros((16, 128), jnp.float32)
    for half in range(2):
        group = jnp.where(f == 1, 3 - (2 * half + c), 2 * half + c)
        piece = jnp.broadcast_to(columns[2 + half], (16, 128))
        piece = spread(jnp.where((lane >> 5) == trc, piece, 0.0))
        ends = jnp.where(((lane >> 5) == group) & (part == to_chip), piece, ends)
    ends = jnp.where(r < 2, ends, jnp.where(holds[2], lines[2], 0.0))
    end_chip = 3 * z
    next_chip = jnp.where(z == 0, x + 1, x - 1)
    for s in range(4):
        rows = jnp.where((next_chip == s) & (c != z), passed, 0.0)
        rows = jnp.where(end_chip == s, ends, rows)
        for j in range(8):
            out_ref[s, WROWS * j + WIN : WROWS * (j + 1)] = rows[2 * j : 2 * j + 2]
    out_ref[x, PASSED:SLOT] = passed
    out_ref[x, KEPT:PASSED] = packet_ref[24:40]


def deposit(slot_ref, total_ref, meta_ref, corner_ref, list_ref, sem):
    t = lax.axis_index("tile")
    first_row = 32 * t
    meta = jnp.concatenate([slot_ref[i // 2, OWN * (i % 2) : OWN * (i % 2) + 1, :] for i in range(8)], 0)
    meta = meta.astype(jnp.int32)
    r = (meta >> 9) - first_row
    meta_ref[...] = jnp.where((r > -(WIN + 1)) & (r < 32), meta, -1)
    copy = pltpu.make_async_copy(meta_ref, corner_ref, sem)
    copy.start()
    total_ref[:, 16:56, :] = jnp.zeros((5, 40, 640), jnp.float32)
    copy.wait()
    count = jnp.int32(0)
    for i in range(32):
        corner = corner_ref[i // 4, META + i % 4]
        list_ref[0, count] = corner
        list_ref[1, count] = i
        count = count + jnp.where(corner >= 0, 1, 0)
    lane = iota((32, 128), 1)
    sub = iota((32, 128), 0)

    def one(n, carry):
        corner = list_ref[0, n]
        i = list_ref[1, n]
        at = (corner >> 9) - first_row + 24
        b = corner & 511
        off = b & 127
        turn = at & 7
        window = slot_ref[i >> 3, pl.ds(pl.multiple_of((i & 7) * WROWS, 8), WROWS), :]
        window = jnp.concatenate([window, jnp.zeros((8, 128), jnp.float32)], 0)
        window = pltpu.roll(window, turn, 0)
        rows = pl.ds(pl.multiple_of((at >> 3) * 8, 8), 32)
        q = (b >> 7) * 128
        here = pl.ds(pl.multiple_of(q, 128), 128)
        there = pl.ds(pl.multiple_of(q + 128, 128), 128)
        inside = (sub >= turn) & (sub < turn + WIN)
        low_side = inside & (lane >= off) & (lane < off + WIN)
        high_side = inside & (lane < off + WIN - 128)
        for m in range(5):
            moved = pltpu.roll(window, (off - WIN * m + 128) % 128, 1)
            total_ref[m, rows, here] += jnp.where(low_side, moved, 0.0)
            total_ref[m, rows, there] += jnp.where(high_side, moved, 0.0)
        return carry

    lax.fori_loop(0, count, one, 0)


def deposited(total_ref, m):
    mass = total_ref[m, 24:56, 0:512]
    spill = pltpu.roll(total_ref[m, 16:56, 512:640], 33, 0)[0:32]
    return jnp.concatenate([mass[:, 0:128] + spill, mass[:, 128:512]], 1)


def halo_sum(slot_ref):
    total = slot_ref[0, SIDES:KEPT]
    ends = None
    for s in range(4):
        rows = jnp.concatenate([slot_ref[s, WROWS * j + WIN : WROWS * (j + 1), :] for j in range(8)], 0)
        ends = rows if s == 0 else ends + rows
        total = total if s == 0 else total + slot_ref[s, SIDES:KEPT]
    return jnp.concatenate([total, ends], 0)


def near_kernel(slot_ref, inner_ref, out_ref, halo_ref, total_ref, meta_ref, corner_ref, list_ref, sem):
    deposit(slot_ref, total_ref, meta_ref, corner_ref, list_ref, sem)
    for m in range(4):
        out_ref[m] = inner_ref[m] + deposited(total_ref, m)
    out_ref[4] = 1.0 + deposited(total_ref, 4)
    halo_ref[...] = halo_sum(slot_ref)


def final_kernel(slot_ref, near_ref, halo_ref, courant_ref, out_ref, total_ref, meta_ref, corner_ref, list_ref, sem):
    _, x, z, c = place_of()
    halo = halo_ref[...] + halo_sum(slot_ref)
    ends = halo[8:24]
    kept = slot_ref[x, KEPT:PASSED]
    passed = slot_ref[x, PASSED:SLOT]
    north = jnp.where(c == 1, kept, jnp.where(z == 0, ends, passed))
    south = jnp.where(c == 0, kept, jnp.where(z == 0, passed, ends))
    west = jnp.where(c == 0, halo[0:1], halo[1:2])
    east = jnp.where(c == 0, halo[2:3], halo[3:4])
    west = jnp.broadcast_to(west, (128, 128)).T
    east = jnp.broadcast_to(east, (128, 128)).T
    deposit(slot_ref, total_ref, meta_ref, corner_ref, list_ref, sem)
    u = courant_ref[0]
    v = courant_ref[1]
    mix = courant_ref[2]
    lane = iota((32, 128), 1)
    first = jnp.where(lane == 0, u[:, 0:128] + mix[:, 0:128], 0.0)
    last = jnp.where(lane == 127, mix[:, 384:512], 0.0)
    line = iota((32, 512), 0)
    above = jnp.where(line == 0, v + mix, 0.0)
    below = jnp.where(line == 31, mix, 0.0)
    scale = 1.0 / (near_ref[4] + deposited(total_ref, 4))
    for m in range(4):
        value = near_ref[m] + deposited(total_ref, m)
        north_row = jnp.concatenate([north[4 * k + m : 4 * k + m + 1] for k in range(4)], 1)
        south_row = jnp.concatenate([south[4 * k + m : 4 * k + m + 1] for k in range(4)], 1)
        value = value + above * north_row + below * south_row
        left = value[:, 0:128] + first * west[32 * m : 32 * m + 32]
        right = value[:, 384:512] + last * east[32 * m : 32 * m + 32]
        out_ref[m] = jnp.concatenate([left, value[:, 128:384], right], 1) * scale


def shape(*dims):
    return jax.ShapeDtypeStruct(dims, jnp.float32)


def dma(n):
    return pltpu.SemaphoreType.DMA((n,))


def cost(bytes_accessed):
    return pl.CostEstimate(flops=bytes_accessed, bytes_accessed=bytes_accessed, transcendentals=0)


def body(parent, courant, edge_links, nest_tracer, nest_weight, nest_map, block_live):
    params = pltpu.CompilerParams(vmem_limit_bytes=32 * 1024 * 1024)
    parent = parent[0, 0]
    courant = courant[0, 0]
    values = nest_tracer[0, :, 0].reshape(4, 4, 32, 128).transpose(0, 2, 1, 3).reshape(4, 128, 128)
    weights = nest_weight[0].reshape(4, 32, 128).transpose(1, 0, 2).reshape(128, 128)
    own, packet = pl.pallas_call(
        pool_kernel,
        out_shape=(shape(ZALL, 128), shape(40, 128)),
        in_specs=[ANY] * 5,
        out_specs=(VMEM, VMEM),
        scratch_shapes=[
            pltpu.VMEM((4, 128, 128), jnp.float32),
            pltpu.VMEM((128, 128), jnp.float32),
            pltpu.VMEM((4, 128), jnp.int32),
            pltpu.SMEM((1, 4), jnp.int32),
            pltpu.VMEM((4, 32, 128), jnp.float32),
            pltpu.VMEM((4, 32, 128), jnp.float32),
            pltpu.VMEM((2, 4, 8, 512), jnp.float32),
            dma(8),
        ],
        compiler_params=params,
    )(*[pltpu.with_memory_space_constraint(a, pltpu.HBM) for a in (values, weights, nest_map[0], parent, block_live)])
    other = lax.ppermute(own, "tile", [(t, t ^ 2) for t in range(16)])
    slots = pl.pallas_call(
        border_kernel,
        out_shape=shape(12, 24, 128),
        in_specs=[VMEM],
        out_specs=VMEM,
        compiler_params=params,
    )(packet)
    lines_of_z = [
        [p * 16 + tile_of(x, z, c) for p in range(6) for z in range(2)] for x in range(4) for c in range(2)
    ]
    slots = lax.all_to_all(slots, ("panel", "tile"), 0, 0, tiled=True, axis_index_groups=lines_of_z)
    inner = pl.pallas_call(
        inner_kernel,
        out_shape=shape(4, 32, 512),
        in_specs=[VMEM, VMEM, ANY],
        out_specs=VMEM,
        compiler_params=params,
        cost_estimate=cost(1 << 24),
    )(parent, courant, other)
    packed = pl.pallas_call(
        pack_kernel,
        out_shape=shape(4, SLOT, 128),
        in_specs=[VMEM, VMEM, VMEM, SMEM, VMEM, ANY],
        out_specs=VMEM,
        compiler_params=params,
    )(own, other, slots, edge_links, packet, inner)
    chips = [[tile_of(x, z, c) for x in range(4)] for z in range(2) for c in range(2)]
    near = lax.all_to_all(packed, "tile", 0, 0, tiled=True, axis_index_groups=chips)
    far = lax.ppermute(near, "tile", [(t, t ^ 1) for t in range(16)])
    scratch = [
        pltpu.VMEM((5, 88, 640), jnp.float32),
        pltpu.VMEM((8, 128), jnp.int32),
        pltpu.SMEM((8, 128), jnp.int32),
        pltpu.SMEM((2, 40), jnp.int32),
        pltpu.SemaphoreType.DMA,
    ]
    summed, halo = pl.pallas_call(
        near_kernel,
        out_shape=(shape(5, 32, 512), shape(24, 128)),
        in_specs=[VMEM, VMEM],
        out_specs=(VMEM, VMEM),
        scratch_shapes=scratch,
        compiler_params=params,
        cost_estimate=cost(1 << 20),
    )(near, inner)
    out = pl.pallas_call(
        final_kernel,
        out_shape=shape(4, 32, 512),
        in_specs=[VMEM, VMEM, VMEM, VMEM],
        out_specs=VMEM,
        scratch_shapes=scratch,
        compiler_params=params,
    )(far, summed, halo, courant)
    return out[None, None]


def solution(mesh):
    placed = (
        P("panel", "lev", None, "tile", None),
        P("panel", "lev", None, "tile", None),
        P(),
        P("panel", "tile", "lev", None, None),
        P("panel", "tile", None),
        P("panel", "tile", None),
        P("panel", "tile"),
    )
    return jax.shard_map(
        body,
        mesh=mesh,
        in_specs=placed,
        out_specs=P("panel", "lev", None, "tile", None),
        check_vma=False,
    )
```

```python
import jax
import jax.numpy as jnp
from jax import lax
from jax.experimental import pallas as pl
from jax.experimental.pallas import tpu as pltpu
from jax.sharding import PartitionSpec as P

WIN = 22
WROWS = 24
FAR = -(64 * 512)
OWN = 4 * WROWS
ZALL = OWN + 8
BOTH = 2 * OWN
SIDES = BOTH
KEPT = SIDES + 8
PASSED = KEPT + 16
SLOT = PASSED + 16
META = 112
LEAD = 10
XLEAD = 2
VMEM = pl.BlockSpec(memory_space=pltpu.VMEM)
SMEM = pl.BlockSpec(memory_space=pltpu.SMEM)
ANY = pl.BlockSpec(memory_space=pl.ANY)


def tile_of(x, z, c):
    return (x * 2 + z) * 2 + c


def place_of():
    t = lax.axis_index("tile")
    return t, t // 4, (t // 2) % 2, t % 2


def lane_rows(line):
    return jnp.concatenate([line[:, 128 * k : 128 * (k + 1)] for k in range(4)], 0)


def three(x):
    hi = x.astype(jnp.bfloat16)
    rest = x - hi.astype(jnp.float32)
    mid = rest.astype(jnp.bfloat16)
    low = (rest - mid.astype(jnp.float32)).astype(jnp.bfloat16)
    return hi, mid, low


def dot(a, b):
    return jnp.dot(a, b, preferred_element_type=jnp.float32)


def dot_exact(a, picks):
    hi, mid, low = three(a)
    return dot(hi, picks) + dot(mid, picks) + dot(low, picks)


def picks_of(mask):
    return mask.astype(jnp.float32).astype(jnp.bfloat16)


def iota(dims, axis):
    return lax.broadcasted_iota(jnp.int32, dims, axis)


def pool_kernel(
    x_hbm, w_hbm, map_hbm, parent_hbm, live_hbm, out_ref, slot_hbm, kept_ref,
    x_ref, w_ref, map_ref, live_ref, west_ref, east_ref, ends_ref, packet_ref, sems
):
    t, _, _, c = place_of()
    copies = [
        pltpu.make_async_copy(parent_hbm.at[:, :, 0:128], west_ref, sems.at[0]),
        pltpu.make_async_copy(parent_hbm.at[:, :, 384:512], east_ref, sems.at[1]),
        pltpu.make_async_copy(parent_hbm.at[:, 0:8, :], ends_ref.at[0], sems.at[2]),
        pltpu.make_async_copy(parent_hbm.at[:, 24:32, :], ends_ref.at[1], sems.at[3]),
        pltpu.make_async_copy(live_hbm, live_ref, sems.at[4]),
        pltpu.make_async_copy(map_hbm.at[:, 0:128], map_ref, sems.at[5]),
        pltpu.make_async_copy(w_hbm, w_ref, sems.at[6]),
        pltpu.make_async_copy(x_hbm, x_ref, sems.at[7]),
    ]
    for copy in copies:
        copy.start()
    for copy in copies[0:4]:
        copy.wait()
    first = lane_rows(ends_ref[0, :, 0, :])
    last = lane_rows(ends_ref[1, :, 7, :])
    west = west_ref[...].reshape(128, 128).T[0:1]
    east = east_ref[...].reshape(128, 128).T[127:128]
    line = jnp.where(t == 0, first, last)
    packet_ref[...] = jnp.concatenate([west, east, jnp.zeros((6, 128), jnp.float32), line], 0)
    sends = [pltpu.make_async_copy(packet_ref, slot_hbm.at[k], sems.at[8 + k]) for k in range(12)]
    for send in sends:
        send.start()
    kept_ref[...] = jnp.where(c == 0, last, first)
    edge = jnp.where(c == 0, first, last)
    for copy in copies[4:6]:
        copy.wait()
    lane = iota((1, 128), 1)
    meta = jnp.zeros((1, 128), jnp.int32)
    for blk in range(4):
        corner = jnp.where(live_ref[0, blk] != 0, map_ref[blk : blk + 1, 0:1], FAR)
        meta = jnp.where(lane == META + blk, corner, meta)
    row = iota((48, 96), 0)
    col = iota((48, 96), 1)
    odd = (row >= WROWS).astype(jnp.int32)
    nest_row = 2 * (col & 31) + odd
    take = picks_of(((nest_row * 43) >> 7) == row - WROWS * odd)
    row = iota((640, 128), 0)
    col = iota((640, 128), 1)
    gather = picks_of((row >> 7) * WIN + (((row & 63) * 43) >> 7) == col)
    for copy in copies[6:8]:
        copy.wait()
    pieces = []
    for blk in range(4):
        live = live_ref[0, blk].astype(jnp.float32)
        weight = w_ref[pl.ds(blk, 32, stride=4), :] * live
        for m in range(4):
            pieces.append(x_ref[blk, pl.ds(m, 32, stride=4), :] * weight)
        pieces.append(weight)
    parts = jnp.concatenate(three(jnp.concatenate(pieces, 1)), 0)
    halves = dot(take, parts)
    wide = iota((WROWS, halves.shape[1]), 1)
    pooled = jnp.where((wide & 64) == 0, halves[:WROWS], halves[WROWS:])
    pooled = jnp.concatenate([pooled[:, 640 * b : 640 * (b + 1)] for b in range(4)], 0)
    out_ref[0:OWN] = dot_exact(pooled, gather)
    out_ref[0:1] = jnp.where(lane < META, out_ref[0:1], meta.astype(jnp.float32))
    for b in range(4):
        out_ref[WROWS * b + WIN : WROWS * (b + 1)] = edge[2 * b : 2 * b + 2]
    out_ref[OWN:ZALL] = edge[8:16]
    for send in sends:
        send.wait()


def inner_kernel(parent_ref, courant_ref, after_ref, out_ref):
    u = courant_ref[0]
    v = courant_ref[1]
    mix = courant_ref[2]
    column = iota((32, 512), 1)
    line = iota((32, 512), 0)
    for m in range(4):
        here = parent_ref[m]
        west = jnp.where(column == 0, 0.0, pltpu.roll(here, 1, 1))
        east = jnp.where(column == 511, 0.0, pltpu.roll(here, 511, 1))
        up = jnp.where(line == 0, 0.0, pltpu.roll(here, 1, 0))
        down = jnp.where(line == 31, 0.0, pltpu.roll(here, 31, 0))
        out_ref[m] = here - u * (here - west) - v * (here - up) + mix * (west + east + up + down - 4.0 * here)


def lines_kernel(slots_ref, links_ref, side_ref, ends_ref):
    _, x, z, c = place_of()
    panel = lax.axis_index("panel")
    sides = (0, 1, 2 + z)
    links = [(links_ref[panel, s, 0], links_ref[panel, s, 1], links_ref[panel, s, 2]) for s in sides]

    def slot_of(q, half):
        return lax.rem(6 * half + q + 12 - LEAD, 12)

    halves = [(0, z ^ links[0][2]), (1, z ^ links[1][2]), (2, 0), (2, 1)]
    columns = []
    for k, half in halves:
        q, r, _ = links[k]
        columns.append(slots_ref[slot_of(q, half), pl.ds(r & 1, 1), :])
    columns = jnp.concatenate(columns + [jnp.zeros((4, 128), jnp.float32)], 0)
    near = iota((128, 128), 0)
    far = iota((128, 128), 1)
    back = dot_exact(columns, picks_of((near ^ 31) == far))
    columns = [jnp.where(links[k][2] == 1, back[i : i + 1], columns[i : i + 1]) for i, (k, _) in enumerate(halves)]
    lines = jnp.concatenate([slots_ref[slot_of(q, r & 1), 8:24, :] for q, r, _ in links], 0)
    back = dot_exact(lines, picks_of((near ^ 127) == far))
    lines = [
        jnp.where(
            links[k][2] == 1,
            jnp.concatenate([back[16 * k + 4 * (3 - p) : 16 * k + 4 * (4 - p)] for p in range(4)], 0),
            lines[16 * k : 16 * (k + 1)],
        )
        for k in range(3)
    ]
    holds = [((r == 2) & (x == 0) & (c == 0)) | ((r == 3) & (x == 3) & (c == 1)) for _, r, _ in links]

    lane = iota((16, 128), 1)
    trc = iota((16, 128), 0) & 3
    part = iota((16, 128), 0) >> 2

    def spread(a):
        return a + pltpu.roll(a, 32, 1) + pltpu.roll(a, 64, 1) + pltpu.roll(a, 96, 1)

    for k in range(2):
        q, r, f = links[k]
        to_chip = jnp.where(f == 1, 3 - x, x)
        to_core = jnp.where(f == 1, 1 - c, c)
        for core in range(2):
            group = 2 * z + core
            cut = jnp.where((lane >> 5) == group, lines[k], 0.0)
            cut = jnp.where((lane >> 5) == trc, spread(cut), 0.0)
            cut = cut + pltpu.roll(cut, 15, 0) + pltpu.roll(cut, 14, 0) + pltpu.roll(cut, 13, 0)
            for s in range(4):
                from_column = jnp.where((to_chip == s) & (to_core == core), columns[k], 0.0)
                from_line = jnp.where(holds[k], cut[4 * s : 4 * s + 1], 0.0)
                at = 2 * k + core
                side_ref[s, at : at + 1] = jnp.where(r < 2, from_column, from_line)

    q, r, f = links[2]
    to_chip = jnp.where(f == 1, 3 - x, x)
    ends = jnp.zeros((16, 128), jnp.float32)
    for half in range(2):
        group = jnp.where(f == 1, 3 - (2 * half + c), 2 * half + c)
        piece = jnp.broadcast_to(columns[2 + half], (16, 128))
        piece = spread(jnp.where((lane >> 5) == trc, piece, 0.0))
        ends = jnp.where(((lane >> 5) == group) & (part == to_chip), piece, ends)
    ends_ref[...] = jnp.where(r < 2, ends, jnp.where(holds[2], lines[2], 0.0))


def pack_kernel(own_ref, other_ref, kept_ref, side_ref, ends_ref, after_ref, out_ref):
    _, x, z, c = place_of()
    passed = jnp.concatenate(
        [other_ref[WROWS * b + WIN : WROWS * (b + 1)] for b in range(4)] + [other_ref[OWN:ZALL]], 0
    )
    end_chip = 3 * z
    next_chip = jnp.where(z == 0, x + 1, x - 1)
    for j in range(4):
        s = (XLEAD + j) % 4
        out_ref[j, 0:OWN] = own_ref[0:OWN]
        out_ref[j, OWN:BOTH] = other_ref[0:OWN]
        out_ref[j, SIDES:KEPT] = side_ref[s]
        rows = jnp.where((next_chip == s) & (c != z), passed, 0.0)
        rows = jnp.where(end_chip == s, ends_ref[...], rows)
        for w in range(8):
            out_ref[j, WROWS * w + WIN : WROWS * (w + 1)] = rows[2 * w : 2 * w + 2]
    here = lax.rem(x + 4 - XLEAD, 4)
    out_ref[here, KEPT:PASSED] = kept_ref[...]
    out_ref[here, PASSED:SLOT] = passed


def deposit(slot_ref, total_ref, meta_ref, corner_ref, list_ref, sem):
    t = lax.axis_index("tile")
    first_row = 32 * t
    meta = jnp.concatenate([slot_ref[i // 2, OWN * (i % 2) : OWN * (i % 2) + 1, :] for i in range(8)], 0)
    meta = meta.astype(jnp.int32)
    r = (meta >> 9) - first_row
    meta_ref[...] = jnp.where((r > -(WIN + 1)) & (r < 32), meta, -1)
    copy = pltpu.make_async_copy(meta_ref, corner_ref, sem)
    copy.start()
    total_ref[:, 16:56, :] = jnp.zeros((5, 40, 640), jnp.float32)
    copy.wait()
    count = jnp.int32(0)
    for i in range(32):
        corner = corner_ref[i // 4, META + i % 4]
        list_ref[0, count] = corner
        list_ref[1, count] = i
        count = count + jnp.where(corner >= 0, 1, 0)
    lane = iota((32, 128), 1)
    sub = iota((32, 128), 0)

    def one(n, carry):
        corner = list_ref[0, n]
        i = list_ref[1, n]
        at = (corner >> 9) - first_row + 24
        b = corner & 511
        off = b & 127
        turn = at & 7
        window = slot_ref[i >> 3, pl.ds(pl.multiple_of((i & 7) * WROWS, 8), WROWS), :]
        window = jnp.concatenate([window, jnp.zeros((8, 128), jnp.float32)], 0)
        window = pltpu.roll(window, turn, 0)
        rows = pl.ds(pl.multiple_of((at >> 3) * 8, 8), 32)
        q = (b >> 7) * 128
        here = pl.ds(pl.multiple_of(q, 128), 128)
        there = pl.ds(pl.multiple_of(q + 128, 128), 128)
        inside = (sub >= turn) & (sub < turn + WIN)
        low_side = inside & (lane >= off) & (lane < off + WIN)
        high_side = inside & (lane < off + WIN - 128)
        for m in range(5):
            moved = pltpu.roll(window, (off - WIN * m + 128) % 128, 1)
            total_ref[m, rows, here] += jnp.where(low_side, moved, 0.0)
            total_ref[m, rows, there] += jnp.where(high_side, moved, 0.0)
        return carry

    lax.fori_loop(0, count, one, 0)


def deposited(total_ref, m):
    mass = total_ref[m, 24:56, 0:512]
    spill = pltpu.roll(total_ref[m, 16:56, 512:640], 33, 0)[0:32]
    return jnp.concatenate([mass[:, 0:128] + spill, mass[:, 128:512]], 1)


def halo_sum(slot_ref):
    total = slot_ref[0, SIDES:KEPT]
    ends = None
    for s in range(4):
        rows = jnp.concatenate([slot_ref[s, WROWS * j + WIN : WROWS * (j + 1), :] for j in range(8)], 0)
        ends = rows if s == 0 else ends + rows
        total = total if s == 0 else total + slot_ref[s, SIDES:KEPT]
    return jnp.concatenate([total, ends], 0)


def near_kernel(slot_ref, inner_ref, out_ref, halo_ref, total_ref, meta_ref, corner_ref, list_ref, sem):
    deposit(slot_ref, total_ref, meta_ref, corner_ref, list_ref, sem)
    for m in range(4):
        out_ref[m] = inner_ref[m] + deposited(total_ref, m)
    out_ref[4] = 1.0 + deposited(total_ref, 4)
    halo_ref[...] = halo_sum(slot_ref)


def final_kernel(slot_ref, near_ref, halo_ref, courant_ref, out_ref, total_ref, meta_ref, corner_ref, list_ref, sem):
    _, x, z, c = place_of()
    halo = halo_ref[...] + halo_sum(slot_ref)
    ends = halo[8:24]
    chip = lax.rem(x + 4 - XLEAD, 4)
    kept = slot_ref[chip, KEPT:PASSED]
    passed = slot_ref[chip, PASSED:SLOT]
    north = jnp.where(c == 1, kept, jnp.where(z == 0, ends, passed))
    south = jnp.where(c == 0, kept, jnp.where(z == 0, passed, ends))
    west = jnp.where(c == 0, halo[0:1], halo[1:2])
    east = jnp.where(c == 0, halo[2:3], halo[3:4])
    west = jnp.broadcast_to(west, (128, 128)).T
    east = jnp.broadcast_to(east, (128, 128)).T
    deposit(slot_ref, total_ref, meta_ref, corner_ref, list_ref, sem)
    u = courant_ref[0]
    v = courant_ref[1]
    mix = courant_ref[2]
    lane = iota((32, 128), 1)
    first = jnp.where(lane == 0, u[:, 0:128] + mix[:, 0:128], 0.0)
    last = jnp.where(lane == 127, mix[:, 384:512], 0.0)
    line = iota((32, 512), 0)
    above = jnp.where(line == 0, v + mix, 0.0)
    below = jnp.where(line == 31, mix, 0.0)
    scale = 1.0 / (near_ref[4] + deposited(total_ref, 4))
    for m in range(4):
        value = near_ref[m] + deposited(total_ref, m)
        north_row = jnp.concatenate([north[4 * k + m : 4 * k + m + 1] for k in range(4)], 1)
        south_row = jnp.concatenate([south[4 * k + m : 4 * k + m + 1] for k in range(4)], 1)
        value = value + above * north_row + below * south_row
        left = value[:, 0:128] + first * west[32 * m : 32 * m + 32]
        right = value[:, 384:512] + last * east[32 * m : 32 * m + 32]
        out_ref[m] = jnp.concatenate([left, value[:, 128:384], right], 1) * scale


def shape(*dims):
    return jax.ShapeDtypeStruct(dims, jnp.float32)


def dma(n):
    return pltpu.SemaphoreType.DMA((n,))


def cost(bytes_accessed):
    return pl.CostEstimate(flops=bytes_accessed, bytes_accessed=bytes_accessed, transcendentals=0)


def body(parent, courant, edge_links, nest_tracer, nest_weight, nest_map, block_live):
    params = pltpu.CompilerParams(vmem_limit_bytes=32 * 1024 * 1024)
    parent = parent[0, 0]
    courant = courant[0, 0]
    values = nest_tracer[0, :, 0].reshape(4, 4, 32, 128).transpose(0, 2, 1, 3).reshape(4, 128, 128)
    weights = nest_weight[0].reshape(4, 32, 128).transpose(1, 0, 2).reshape(128, 128)
    own, slots, kept = pl.pallas_call(
        pool_kernel,
        out_shape=(shape(ZALL, 128), shape(12, 24, 128), shape(16, 128)),
        in_specs=[ANY] * 5,
        out_specs=(VMEM, ANY, VMEM),
        scratch_shapes=[
            pltpu.VMEM((4, 128, 128), jnp.float32),
            pltpu.VMEM((128, 128), jnp.float32),
            pltpu.VMEM((4, 128), jnp.int32),
            pltpu.SMEM((1, 4), jnp.int32),
            pltpu.VMEM((4, 32, 128), jnp.float32),
            pltpu.VMEM((4, 32, 128), jnp.float32),
            pltpu.VMEM((2, 4, 8, 512), jnp.float32),
            pltpu.VMEM((24, 128), jnp.float32),
            dma(20),
        ],
        compiler_params=params,
    )(*[pltpu.with_memory_space_constraint(a, pltpu.HBM) for a in (values, weights, nest_map[0], parent, block_live)])
    other = lax.ppermute(own, "tile", [(t, t ^ 2) for t in range(16)])
    around = [(LEAD + j) % 12 for j in range(12)]
    lines_of_z = [
        [(zz % 6) * 16 + tile_of(x, zz // 6, c) for zz in around] for x in range(4) for c in range(2)
    ]
    slots = lax.all_to_all(slots, ("panel", "tile"), 0, 0, tiled=True, axis_index_groups=lines_of_z)
    side, ends = pl.pallas_call(
        lines_kernel,
        out_shape=(shape(4, 8, 128), shape(16, 128)),
        in_specs=[VMEM, SMEM],
        out_specs=(VMEM, VMEM),
        compiler_params=params,
    )(slots, edge_links)
    inner = pl.pallas_call(
        inner_kernel,
        out_shape=shape(4, 32, 512),
        in_specs=[VMEM, VMEM, ANY],
        out_specs=VMEM,
        compiler_params=params,
        cost_estimate=cost(1 << 20),
    )(parent, courant, own)
    packed = pl.pallas_call(
        pack_kernel,
        out_shape=shape(4, SLOT, 128),
        in_specs=[VMEM, VMEM, VMEM, VMEM, VMEM, ANY],
        out_specs=VMEM,
        compiler_params=params,
    )(own, other, kept, side, ends, inner)
    chips = [[tile_of((XLEAD + j) % 4, z, c) for j in range(4)] for z in range(2) for c in range(2)]
    near = lax.all_to_all(packed, "tile", 0, 0, tiled=True, axis_index_groups=chips)
    far = lax.ppermute(near, "tile", [(t, t ^ 1) for t in range(16)])
    scratch = [
        pltpu.VMEM((5, 88, 640), jnp.float32),
        pltpu.VMEM((8, 128), jnp.int32),
        pltpu.SMEM((8, 128), jnp.int32),
        pltpu.SMEM((2, 40), jnp.int32),
        pltpu.SemaphoreType.DMA,
    ]
    summed, halo = pl.pallas_call(
        near_kernel,
        out_shape=(shape(5, 32, 512), shape(24, 128)),
        in_specs=[VMEM, VMEM],
        out_specs=(VMEM, VMEM),
        scratch_shapes=scratch,
        compiler_params=params,
        cost_estimate=cost(1 << 20),
    )(near, inner)
    out = pl.pallas_call(
        final_kernel,
        out_shape=shape(4, 32, 512),
        in_specs=[VMEM, VMEM, VMEM, VMEM],
        out_specs=VMEM,
        scratch_shapes=scratch,
        compiler_params=params,
    )(far, summed, halo, courant)
    return out[None, None]


def solution(mesh):
    placed = (
        P("panel", "lev", None, "tile", None),
        P("panel", "lev", None, "tile", None),
        P(),
        P("panel", "tile", "lev", None, None),
        P("panel", "tile", None),
        P("panel", "tile", None),
        P("panel", "tile"),
    )
    return jax.shard_map(
        body,
        mesh=mesh,
        in_specs=placed,
        out_specs=P("panel", "lev", None, "tile", None),
        check_vma=False,
    )
```

```python
import jax
import jax.numpy as jnp
from jax import lax
from jax.experimental import pallas as pl
from jax.experimental.pallas import tpu as pltpu
from jax.sharding import PartitionSpec as P

WIN = 22
WROWS = 24
FAR = -(64 * 512)
OWN = 4 * WROWS
SLOT = 2 * OWN
META = 110
FREE = 112
LEAD = 10
XLEAD = 2
VMEM = pl.BlockSpec(memory_space=pltpu.VMEM)
SMEM = pl.BlockSpec(memory_space=pltpu.SMEM)
ANY = pl.BlockSpec(memory_space=pl.ANY)


def tile_of(x, z, c):
    return (x * 2 + z) * 2 + c


def place_of():
    t = lax.axis_index("tile")
    return t, t // 4, (t // 2) % 2, t % 2


def lane_rows(line):
    return jnp.concatenate([line[:, 128 * k : 128 * (k + 1)] for k in range(4)], 0)


def three(x):
    hi = x.astype(jnp.bfloat16)
    rest = x - hi.astype(jnp.float32)
    mid = rest.astype(jnp.bfloat16)
    low = (rest - mid.astype(jnp.float32)).astype(jnp.bfloat16)
    return hi, mid, low


def dot(a, b):
    return jnp.dot(a, b, preferred_element_type=jnp.float32)


def dot_exact(a, picks):
    hi, mid, low = three(a)
    return dot(hi, picks) + dot(mid, picks) + dot(low, picks)


def picks_of(mask):
    return mask.astype(jnp.float32).astype(jnp.bfloat16)


def iota(dims, axis):
    return lax.broadcasted_iota(jnp.int32, dims, axis)


def to_free(rows, g):
    return pltpu.roll(rows, (FREE - 16 * g) % 128, 1)


def from_free(parts):
    lane = iota(parts[0].shape, 1) >> 4
    rows = jnp.zeros_like(parts[0])
    for g in range(8):
        rows = jnp.where(lane == g, pltpu.roll(parts[g], (16 * g - FREE + 128) % 128, 1), rows)
    return rows


def pool_kernel(
    x_hbm, w_hbm, map_hbm, parent_hbm, live_hbm, out_ref, slot_hbm, kept_ref,
    x_ref, w_ref, map_ref, live_ref, parent_ref, packet_ref, sems
):
    t, _, _, c = place_of()
    copies = [
        pltpu.make_async_copy(parent_hbm, parent_ref, sems.at[0]),
        pltpu.make_async_copy(live_hbm, live_ref, sems.at[1]),
        pltpu.make_async_copy(map_hbm.at[:, 0:128], map_ref, sems.at[2]),
        pltpu.make_async_copy(w_hbm, w_ref, sems.at[3]),
        pltpu.make_async_copy(x_hbm, x_ref, sems.at[4]),
    ]
    for copy in copies:
        copy.start()
    copies[0].wait()
    first = parent_ref[:, 0, :]
    last = parent_ref[:, 31, :]
    west = parent_ref[:, :, 0:128].reshape(128, 128).T[0:1]
    east = parent_ref[:, :, 384:512].reshape(128, 128).T[127:128]
    line = jnp.where(t == 0, first, last)
    packet = jnp.concatenate([west, east, jnp.zeros((6, 128), jnp.float32), lane_rows(line)], 0)
    for k in range(12):
        packet_ref[k] = packet
    send = pltpu.make_async_copy(packet_ref, slot_hbm, sems.at[5])
    send.start()
    first = lane_rows(first)
    last = lane_rows(last)
    kept_ref[...] = jnp.where(c == 0, last, first)
    edge = jnp.where(c == 0, first, last)
    for copy in copies[1:3]:
        copy.wait()
    row = iota((48, 96), 0)
    col = iota((48, 96), 1)
    odd = (row >= WROWS).astype(jnp.int32)
    nest_row = 2 * (col & 31) + odd
    take = picks_of(((nest_row * 43) >> 7) == row - WROWS * odd)
    row = iota((640, 128), 0)
    col = iota((640, 128), 1)
    gather = picks_of((row >> 7) * WIN + (((row & 63) * 43) >> 7) == col)
    for copy in copies[3:5]:
        copy.wait()
    pieces = []
    for blk in range(4):
        live = live_ref[0, blk].astype(jnp.float32)
        weight = w_ref[pl.ds(blk, 32, stride=4), :] * live
        for m in range(4):
            pieces.append(x_ref[blk, pl.ds(m, 32, stride=4), :] * weight)
        pieces.append(weight)
    parts = jnp.concatenate(three(jnp.concatenate(pieces, 1)), 0)
    halves = dot(take, parts)
    wide = iota((WROWS, halves.shape[1]), 1)
    pooled = jnp.where((wide & 64) == 0, halves[:WROWS], halves[WROWS:])
    pooled = jnp.concatenate([pooled[:, 640 * b : 640 * (b + 1)] for b in range(4)], 0)
    windows = dot_exact(pooled, gather)
    rest = jnp.zeros((8, 128), jnp.float32)
    extra = [e for b in range(4) for e in (to_free(edge[8:16], 2 * b), to_free(edge[8:16], 2 * b + 1), rest)]
    lane = iota((OWN, 128), 1)
    out_ref[...] = jnp.where(lane < FREE, windows, jnp.concatenate(extra, 0))
    lane = iota((1, 128), 1)
    for k in range(2):
        row = out_ref[k : k + 1]
        for e in range(2):
            blk = 2 * k + e
            corner = jnp.where(live_ref[0, blk] != 0, map_ref[blk : blk + 1, 0:1], FAR)
            row = jnp.where(lane == META + e, corner.astype(jnp.float32), row)
        out_ref[k : k + 1] = row
    for b in range(4):
        out_ref[WROWS * b + WIN : WROWS * (b + 1)] = edge[2 * b : 2 * b + 2]
    send.wait()


def inner_kernel(parent_ref, courant_ref, after_ref, out_ref):
    u = courant_ref[0]
    v = courant_ref[1]
    mix = courant_ref[2]
    column = iota((32, 512), 1)
    line = iota((32, 512), 0)
    for m in range(4):
        here = parent_ref[m]
        west = jnp.where(column == 0, 0.0, pltpu.roll(here, 1, 1))
        east = jnp.where(column == 511, 0.0, pltpu.roll(here, 511, 1))
        up = jnp.where(line == 0, 0.0, pltpu.roll(here, 1, 0))
        down = jnp.where(line == 31, 0.0, pltpu.roll(here, 31, 0))
        out_ref[m] = here - u * (here - west) - v * (here - up) + mix * (west + east + up + down - 4.0 * here)


def lines_kernel(slots_ref, links_ref, side_ref, ends_ref):
    _, x, z, c = place_of()
    panel = lax.axis_index("panel")
    sides = (0, 1, 2 + z)
    links = [(links_ref[panel, s, 0], links_ref[panel, s, 1], links_ref[panel, s, 2]) for s in sides]

    def slot_of(q, half):
        return lax.rem(6 * half + q + 12 - LEAD, 12)

    halves = [(0, z ^ links[0][2]), (1, z ^ links[1][2]), (2, 0), (2, 1)]
    columns = []
    for k, half in halves:
        q, r, _ = links[k]
        columns.append(slots_ref[slot_of(q, half), pl.ds(r & 1, 1), :])
    columns = jnp.concatenate(columns + [jnp.zeros((4, 128), jnp.float32)], 0)
    near = iota((128, 128), 0)
    far = iota((128, 128), 1)
    back = dot_exact(columns, picks_of((near ^ 31) == far))
    columns = [jnp.where(links[k][2] == 1, back[i : i + 1], columns[i : i + 1]) for i, (k, _) in enumerate(halves)]
    lines = jnp.concatenate([slots_ref[slot_of(q, r & 1), 8:24, :] for q, r, _ in links], 0)
    back = dot_exact(lines, picks_of((near ^ 127) == far))
    lines = [
        jnp.where(
            links[k][2] == 1,
            jnp.concatenate([back[16 * k + 4 * (3 - p) : 16 * k + 4 * (4 - p)] for p in range(4)], 0),
            lines[16 * k : 16 * (k + 1)],
        )
        for k in range(3)
    ]
    holds = [((r == 2) & (x == 0) & (c == 0)) | ((r == 3) & (x == 3) & (c == 1)) for _, r, _ in links]

    lane = iota((16, 128), 1)
    trc = iota((16, 128), 0) & 3
    part = iota((16, 128), 0) >> 2

    def spread(a):
        return a + pltpu.roll(a, 32, 1) + pltpu.roll(a, 64, 1) + pltpu.roll(a, 96, 1)

    for k in range(2):
        q, r, f = links[k]
        to_chip = jnp.where(f == 1, 3 - x, x)
        to_core = jnp.where(f == 1, 1 - c, c)
        for core in range(2):
            group = 2 * z + core
            cut = jnp.where((lane >> 5) == group, lines[k], 0.0)
            cut = jnp.where((lane >> 5) == trc, spread(cut), 0.0)
            cut = cut + pltpu.roll(cut, 15, 0) + pltpu.roll(cut, 14, 0) + pltpu.roll(cut, 13, 0)
            for s in range(4):
                from_column = jnp.where((to_chip == s) & (to_core == core), columns[k], 0.0)
                from_line = jnp.where(holds[k], cut[4 * s : 4 * s + 1], 0.0)
                at = 2 * k + core
                side_ref[s, at : at + 1] = jnp.where(r < 2, from_column, from_line)

    q, r, f = links[2]
    to_chip = jnp.where(f == 1, 3 - x, x)
    ends = jnp.zeros((16, 128), jnp.float32)
    for half in range(2):
        group = jnp.where(f == 1, 3 - (2 * half + c), 2 * half + c)
        piece = jnp.broadcast_to(columns[2 + half], (16, 128))
        piece = spread(jnp.where((lane >> 5) == trc, piece, 0.0))
        ends = jnp.where(((lane >> 5) == group) & (part == to_chip), piece, ends)
    ends_ref[...] = jnp.where(r < 2, ends, jnp.where(holds[2], lines[2], 0.0))


def pack_kernel(own_ref, other_ref, kept_ref, side_ref, ends_ref, after_ref, out_ref):
    _, x, z, c = place_of()
    passed = from_free([other_ref[WROWS * (g // 2) + 8 * (g % 2) : WROWS * (g // 2) + 8 * (g % 2) + 8] for g in range(8)])
    passed = jnp.concatenate([other_ref[WROWS * b + WIN : WROWS * (b + 1)] for b in range(4)] + [passed], 0)
    kept = kept_ref[...]
    ends = ends_ref[...]
    high = iota((16, 128), 1) < FREE
    low = iota((8, 128), 1) < FREE
    end_chip = 3 * z
    next_chip = jnp.where(z == 0, x + 1, x - 1)
    for j in range(4):
        s = (XLEAD + j) % 4
        side = side_ref[s]
        rows = jnp.where((next_chip == s) & (c != z), passed, 0.0)
        rows = jnp.where(end_chip == s, ends, rows)
        rows = jnp.where((x == s) & (c == z), passed, rows)
        for w in range(8):
            window_ref = own_ref if w < 4 else other_ref
            at = WROWS * (w % 4)
            to = WROWS * w
            out_ref[j, to : to + 16] = jnp.where(high, window_ref[at : at + 16], to_free(kept, w))
            out_ref[j, to + 16 : to + 24] = jnp.where(low, window_ref[at + 16 : at + 24], to_free(side, w))
            out_ref[j, to + WIN : to + WROWS] = rows[2 * w : 2 * w + 2]


def halo_sum(slot_ref, skip):
    sides = []
    for w in range(8):
        at = WROWS * w + 16
        sides.append(slot_ref[0, at : at + 8] + slot_ref[1, at : at + 8] + slot_ref[2, at : at + 8] + slot_ref[3, at : at + 8])
    ends = jnp.zeros((16, 128), jnp.float32)
    for s in range(4):
        rows = jnp.concatenate([slot_ref[s, WROWS * w + WIN : WROWS * (w + 1), :] for w in range(8)], 0)
        ends = ends + jnp.where(skip == s, 0.0, rows)
    return jnp.concatenate([from_free(sides), ends], 0)


def deposit_start(slot_ref, total_ref, meta_ref, corner_ref, sem):
    first_row = 32 * lax.axis_index("tile")
    meta = jnp.concatenate([slot_ref[i // 2, OWN * (i % 2) : OWN * (i % 2) + 2, :] for i in range(8)], 0)
    meta = meta.astype(jnp.int32)
    r = (meta >> 9) - first_row
    meta_ref[...] = jnp.where((r > -(WIN + 1)) & (r < 32), meta, -1)
    copy = pltpu.make_async_copy(meta_ref, corner_ref, sem)
    copy.start()
    total_ref[:, 16:56, :] = jnp.zeros((5, 40, 640), jnp.float32)
    return copy


def deposit(slot_ref, total_ref, corner_ref, list_ref):
    first_row = 32 * lax.axis_index("tile")
    count = jnp.int32(0)
    for i in range(32):
        corner = corner_ref[i // 2, META + i % 2]
        list_ref[0, count] = corner
        list_ref[1, count] = i
        count = count + jnp.where(corner >= 0, 1, 0)
    lane = iota((32, 128), 1)
    sub = iota((32, 128), 0)

    def one(n, carry):
        corner = list_ref[0, n]
        i = list_ref[1, n]
        at = (corner >> 9) - first_row + 24
        b = corner & 511
        off = b & 127
        turn = at & 7
        window = slot_ref[i >> 3, pl.ds(pl.multiple_of((i & 7) * WROWS, 8), WROWS), :]
        window = jnp.concatenate([window, jnp.zeros((8, 128), jnp.float32)], 0)
        window = pltpu.roll(window, turn, 0)
        rows = pl.ds(pl.multiple_of((at >> 3) * 8, 8), 32)
        q = (b >> 7) * 128
        here = pl.ds(pl.multiple_of(q, 128), 128)
        there = pl.ds(pl.multiple_of(q + 128, 128), 128)
        inside = (sub >= turn) & (sub < turn + WIN)
        low_side = inside & (lane >= off) & (lane < off + WIN)
        high_side = inside & (lane < off + WIN - 128)
        for m in range(5):
            moved = pltpu.roll(window, (off - WIN * m + 128) % 128, 1)
            total_ref[m, rows, here] += jnp.where(low_side, moved, 0.0)
            total_ref[m, rows, there] += jnp.where(high_side, moved, 0.0)
        return carry

    lax.fori_loop(0, count, one, 0)


def deposited(total_ref, m):
    mass = total_ref[m, 24:56, 0:512]
    spill = pltpu.roll(total_ref[m, 16:56, 512:640], 33, 0)[0:32]
    return jnp.concatenate([mass[:, 0:128] + spill, mass[:, 128:512]], 1)


def near_kernel(slot_ref, inner_ref, end_ref, out_ref, halo_ref, total_ref, meta_ref, corner_ref, list_ref, sem):
    _, x, z, c = place_of()
    copy = deposit_start(slot_ref, total_ref, meta_ref, corner_ref, sem)
    halo = halo_sum(slot_ref, lax.rem(x + 4 - XLEAD, 4))
    halo_ref[0:8] = halo[0:8]
    halo_ref[8:24] = halo[8:24] + jnp.where((x == 3 * z) & (c == z), end_ref[...], 0.0)
    copy.wait()
    deposit(slot_ref, total_ref, corner_ref, list_ref)
    for m in range(4):
        out_ref[m] = inner_ref[m] + deposited(total_ref, m)
    out_ref[4] = 1.0 + deposited(total_ref, 4)


def final_kernel(slot_ref, near_ref, halo_ref, courant_ref, out_ref, total_ref, meta_ref, corner_ref, list_ref, sem):
    _, x, z, c = place_of()
    copy = deposit_start(slot_ref, total_ref, meta_ref, corner_ref, sem)
    halo = halo_ref[...] + halo_sum(slot_ref, -1)
    chip = lax.rem(x + 4 - XLEAD, 4)
    kept = from_free([slot_ref[chip, WROWS * w : WROWS * w + 16, :] for w in range(8)])
    passed = jnp.concatenate([slot_ref[chip, WROWS * w + WIN : WROWS * (w + 1), :] for w in range(8)], 0)
    crossing = jnp.where(c == z, halo[8:24], passed)
    north = jnp.where(c == 0, crossing, kept)
    south = jnp.where(c == 0, kept, crossing)
    west = jnp.where(c == 0, halo[0:1], halo[1:2])
    east = jnp.where(c == 0, halo[2:3], halo[3:4])
    west = jnp.broadcast_to(west, (128, 128)).T
    east = jnp.broadcast_to(east, (128, 128)).T
    v = courant_ref[1]
    mix = courant_ref[2]
    lane = iota((32, 128), 1)
    first = jnp.where(lane == 0, courant_ref[0, :, 0:128] + mix[:, 0:128], 0.0)
    last = jnp.where(lane == 127, mix[:, 384:512], 0.0)
    line = iota((32, 512), 0)
    above = jnp.where(line == 0, v + mix, 0.0)
    below = jnp.where(line == 31, mix, 0.0)
    for m in range(4):
        value = near_ref[m]
        north_row = jnp.concatenate([north[4 * k + m : 4 * k + m + 1] for k in range(4)], 1)
        south_row = jnp.concatenate([south[4 * k + m : 4 * k + m + 1] for k in range(4)], 1)
        value = value + above * north_row + below * south_row
        left = value[:, 0:128] + first * west[32 * m : 32 * m + 32]
        right = value[:, 384:512] + last * east[32 * m : 32 * m + 32]
        out_ref[m] = jnp.concatenate([left, value[:, 128:384], right], 1)
    copy.wait()
    deposit(slot_ref, total_ref, corner_ref, list_ref)
    scale = 1.0 / (near_ref[4] + deposited(total_ref, 4))
    for m in range(4):
        out_ref[m] = (out_ref[m] + deposited(total_ref, m)) * scale


def shape(*dims):
    return jax.ShapeDtypeStruct(dims, jnp.float32)


def dma(n):
    return pltpu.SemaphoreType.DMA((n,))


def cost(bytes_accessed):
    return pl.CostEstimate(flops=bytes_accessed, bytes_accessed=bytes_accessed, transcendentals=0)


def body(parent, courant, edge_links, nest_tracer, nest_weight, nest_map, block_live):
    params = pltpu.CompilerParams(vmem_limit_bytes=32 * 1024 * 1024)
    parent = parent[0, 0]
    courant = courant[0, 0]
    values = nest_tracer[0, :, 0].reshape(4, 4, 32, 128).transpose(0, 2, 1, 3).reshape(4, 128, 128)
    weights = nest_weight[0].reshape(4, 32, 128).transpose(1, 0, 2).reshape(128, 128)
    own, slots, kept = pl.pallas_call(
        pool_kernel,
        out_shape=(shape(OWN, 128), shape(12, 24, 128), shape(16, 128)),
        in_specs=[ANY] * 5,
        out_specs=(VMEM, ANY, VMEM),
        scratch_shapes=[
            pltpu.VMEM((4, 128, 128), jnp.float32),
            pltpu.VMEM((128, 128), jnp.float32),
            pltpu.VMEM((4, 128), jnp.int32),
            pltpu.SMEM((1, 4), jnp.int32),
            pltpu.VMEM((4, 32, 512), jnp.float32),
            pltpu.VMEM((12, 24, 128), jnp.float32),
            dma(6),
        ],
        compiler_params=params,
    )(*[pltpu.with_memory_space_constraint(a, pltpu.HBM) for a in (values, weights, nest_map[0], parent, block_live)])
    other = lax.ppermute(own, "tile", [(t, t ^ 2) for t in range(16)])
    around = [(LEAD + j) % 12 for j in range(12)]
    lines_of_z = [
        [(zz % 6) * 16 + tile_of(x, zz // 6, c) for zz in around] for x in range(4) for c in range(2)
    ]
    slots = lax.all_to_all(slots, ("panel", "tile"), 0, 0, tiled=True, axis_index_groups=lines_of_z)
    side, ends = pl.pallas_call(
        lines_kernel,
        out_shape=(shape(4, 8, 128), shape(16, 128)),
        in_specs=[VMEM, SMEM],
        out_specs=(VMEM, VMEM),
        compiler_params=params,
    )(slots, edge_links)
    inner = pl.pallas_call(
        inner_kernel,
        out_shape=shape(4, 32, 512),
        in_specs=[VMEM, VMEM, ANY],
        out_specs=VMEM,
        compiler_params=params,
        cost_estimate=cost(1 << 20),
    )(parent, courant, own)
    packed = pl.pallas_call(
        pack_kernel,
        out_shape=shape(4, SLOT, 128),
        in_specs=[VMEM, VMEM, VMEM, VMEM, VMEM, ANY],
        out_specs=VMEM,
        compiler_params=params,
    )(own, other, kept, side, ends, inner)
    chips = [[tile_of((XLEAD + j) % 4, z, c) for j in range(4)] for z in range(2) for c in range(2)]
    near = lax.all_to_all(packed, "tile", 0, 0, tiled=True, axis_index_groups=chips)
    far = lax.ppermute(near, "tile", [(t, t ^ 1) for t in range(16)])
    scratch = [
        pltpu.VMEM((5, 88, 640), jnp.float32),
        pltpu.VMEM((16, 128), jnp.int32),
        pltpu.SMEM((16, 128), jnp.int32),
        pltpu.SMEM((2, 40), jnp.int32),
        pltpu.SemaphoreType.DMA,
    ]
    summed, halo = pl.pallas_call(
        near_kernel,
        out_shape=(shape(5, 32, 512), shape(24, 128)),
        in_specs=[VMEM, VMEM, VMEM],
        out_specs=(VMEM, VMEM),
        scratch_shapes=scratch,
        compiler_params=params,
        cost_estimate=cost(1 << 20),
    )(near, inner, ends)
    out = pl.pallas_call(
        final_kernel,
        out_shape=shape(4, 32, 512),
        in_specs=[VMEM, VMEM, VMEM, VMEM],
        out_specs=VMEM,
        scratch_shapes=scratch,
        compiler_params=params,
    )(far, summed, halo, courant)
    return out[None, None]


def solution(mesh):
    placed = (
        P("panel", "lev", None, "tile", None),
        P("panel", "lev", None, "tile", None),
        P(),
        P("panel", "tile", "lev", None, None),
        P("panel", "tile", None),
        P("panel", "tile", None),
        P("panel", "tile"),
    )
    return jax.shard_map(
        body,
        mesh=mesh,
        in_specs=placed,
        out_specs=P("panel", "lev", None, "tile", None),
        check_vma=False,
    )
```

```python
import jax
import jax.numpy as jnp
from jax import lax
from jax.experimental import pallas as pl
from jax.experimental.pallas import tpu as pltpu
from jax.sharding import PartitionSpec as P

WIN = 22
WROWS = 24
FAR = -(64 * 512)
OWN = 4 * WROWS
SLOT = 2 * OWN
META = 110
FREE = 112
LEAD = 10
XLEAD = 2
VMEM = pl.BlockSpec(memory_space=pltpu.VMEM)
SMEM = pl.BlockSpec(memory_space=pltpu.SMEM)
ANY = pl.BlockSpec(memory_space=pl.ANY)


def tile_of(x, z, c):
    return (x * 2 + z) * 2 + c


def place_of():
    t = lax.axis_index("tile")
    return t, t // 4, (t // 2) % 2, t % 2


def lane_rows(line):
    return jnp.concatenate([line[:, 128 * k : 128 * (k + 1)] for k in range(4)], 0)


def three(x):
    hi = x.astype(jnp.bfloat16)
    rest = x - hi.astype(jnp.float32)
    mid = rest.astype(jnp.bfloat16)
    low = (rest - mid.astype(jnp.float32)).astype(jnp.bfloat16)
    return hi, mid, low


def dot(a, b):
    return jnp.dot(a, b, preferred_element_type=jnp.float32)


def dot_exact(a, picks):
    hi, mid, low = three(a)
    return dot(hi, picks) + dot(mid, picks) + dot(low, picks)


def picks_of(mask):
    return mask.astype(jnp.float32).astype(jnp.bfloat16)


def iota(dims, axis):
    return lax.broadcasted_iota(jnp.int32, dims, axis)


def to_free(rows, g):
    return pltpu.roll(rows, (FREE - 16 * g) % 128, 1)


def from_free(parts):
    lane = iota(parts[0].shape, 1) >> 4
    rows = jnp.zeros_like(parts[0])
    for g in range(8):
        rows = jnp.where(lane == g, pltpu.roll(parts[g], (16 * g - FREE + 128) % 128, 1), rows)
    return rows


def pool_kernel(
    x_hbm, w_hbm, map_hbm, parent_hbm, live_hbm, out_ref, slot_hbm, kept_ref,
    x_ref, w_ref, map_ref, live_ref, parent_ref, packet_ref, sems
):
    t, _, _, c = place_of()
    copies = [
        pltpu.make_async_copy(parent_hbm, parent_ref, sems.at[0]),
        pltpu.make_async_copy(live_hbm, live_ref, sems.at[1]),
        pltpu.make_async_copy(map_hbm.at[:, 0:128], map_ref, sems.at[2]),
        pltpu.make_async_copy(w_hbm, w_ref, sems.at[3]),
        pltpu.make_async_copy(x_hbm, x_ref, sems.at[4]),
    ]
    for copy in copies:
        copy.start()
    copies[0].wait()
    first = parent_ref[:, 0, :]
    last = parent_ref[:, 31, :]
    west = parent_ref[:, :, 0:128].reshape(128, 128).T[0:1]
    east = parent_ref[:, :, 384:512].reshape(128, 128).T[127:128]
    line = jnp.where(t == 0, first, last)
    packet = jnp.concatenate([west, east, jnp.zeros((6, 128), jnp.float32), lane_rows(line)], 0)
    for k in range(12):
        packet_ref[k] = packet
    send = pltpu.make_async_copy(packet_ref, slot_hbm, sems.at[5])
    send.start()
    first = lane_rows(first)
    last = lane_rows(last)
    kept_ref[...] = jnp.where(c == 0, last, first)
    edge = jnp.where(c == 0, first, last)
    for copy in copies[1:3]:
        copy.wait()
    row = iota((48, 96), 0)
    col = iota((48, 96), 1)
    odd = (row >= WROWS).astype(jnp.int32)
    nest_row = 2 * (col & 31) + odd
    take = picks_of(((nest_row * 43) >> 7) == row - WROWS * odd)
    row = iota((640, 128), 0)
    col = iota((640, 128), 1)
    gather = picks_of((row >> 7) * WIN + (((row & 63) * 43) >> 7) == col)
    for copy in copies[3:5]:
        copy.wait()
    pieces = []
    for blk in range(4):
        live = live_ref[0, blk].astype(jnp.float32)
        weight = w_ref[pl.ds(blk, 32, stride=4), :] * live
        for m in range(4):
            pieces.append(x_ref[blk, pl.ds(m, 32, stride=4), :] * weight)
        pieces.append(weight)
    parts = jnp.concatenate(three(jnp.concatenate(pieces, 1)), 0)
    halves = dot(take, parts)
    wide = iota((WROWS, halves.shape[1]), 1)
    pooled = jnp.where((wide & 64) == 0, halves[:WROWS], halves[WROWS:])
    pooled = jnp.concatenate([pooled[:, 640 * b : 640 * (b + 1)] for b in range(4)], 0)
    windows = dot_exact(pooled, gather)
    rest = jnp.zeros((8, 128), jnp.float32)
    extra = [e for b in range(4) for e in (to_free(edge[8:16], 2 * b), to_free(edge[8:16], 2 * b + 1), rest)]
    lane = iota((OWN, 128), 1)
    out_ref[...] = jnp.where(lane < FREE, windows, jnp.concatenate(extra, 0))
    lane = iota((1, 128), 1)
    for k in range(2):
        row = out_ref[k : k + 1]
        for e in range(2):
            blk = 2 * k + e
            corner = jnp.where(live_ref[0, blk] != 0, map_ref[blk : blk + 1, 0:1], FAR)
            row = jnp.where(lane == META + e, corner.astype(jnp.float32), row)
        out_ref[k : k + 1] = row
    for b in range(4):
        out_ref[WROWS * b + WIN : WROWS * (b + 1)] = edge[2 * b : 2 * b + 2]
    send.wait()


def inner_kernel(parent_ref, courant_ref, after_ref, out_ref):
    u = courant_ref[0]
    v = courant_ref[1]
    mix = courant_ref[2]
    column = iota((32, 512), 1)
    line = iota((32, 512), 0)
    for m in range(4):
        here = parent_ref[m]
        west = jnp.where(column == 0, 0.0, pltpu.roll(here, 1, 1))
        east = jnp.where(column == 511, 0.0, pltpu.roll(here, 511, 1))
        up = jnp.where(line == 0, 0.0, pltpu.roll(here, 1, 0))
        down = jnp.where(line == 31, 0.0, pltpu.roll(here, 31, 0))
        out_ref[m] = here - u * (here - west) - v * (here - up) + mix * (west + east + up + down - 4.0 * here)


def lines_kernel(slots_ref, links_ref, side_ref, ends_ref):
    _, x, z, c = place_of()
    panel = lax.axis_index("panel")
    sides = (0, 1, 2 + z)
    links = [(links_ref[panel, s, 0], links_ref[panel, s, 1], links_ref[panel, s, 2]) for s in sides]

    def slot_of(q, half):
        return lax.rem(6 * half + q + 12 - LEAD, 12)

    halves = [(0, z ^ links[0][2]), (1, z ^ links[1][2]), (2, 0), (2, 1)]
    columns = []
    for k, half in halves:
        q, r, _ = links[k]
        columns.append(slots_ref[slot_of(q, half), pl.ds(r & 1, 1), :])
    columns = jnp.concatenate(columns + [jnp.zeros((4, 128), jnp.float32)], 0)
    near = iota((128, 128), 0)
    far = iota((128, 128), 1)
    back = dot_exact(columns, picks_of((near ^ 31) == far))
    columns = [jnp.where(links[k][2] == 1, back[i : i + 1], columns[i : i + 1]) for i, (k, _) in enumerate(halves)]
    lines = jnp.concatenate([slots_ref[slot_of(q, r & 1), 8:24, :] for q, r, _ in links], 0)
    back = dot_exact(lines, picks_of((near ^ 127) == far))
    lines = [
        jnp.where(
            links[k][2] == 1,
            jnp.concatenate([back[16 * k + 4 * (3 - p) : 16 * k + 4 * (4 - p)] for p in range(4)], 0),
            lines[16 * k : 16 * (k + 1)],
        )
        for k in range(3)
    ]
    holds = [((r == 2) & (x == 0) & (c == 0)) | ((r == 3) & (x == 3) & (c == 1)) for _, r, _ in links]

    lane = iota((16, 128), 1)
    trc = iota((16, 128), 0) & 3
    part = iota((16, 128), 0) >> 2

    def spread(a):
        return a + pltpu.roll(a, 32, 1) + pltpu.roll(a, 64, 1) + pltpu.roll(a, 96, 1)

    for k in range(2):
        q, r, f = links[k]
        to_chip = jnp.where(f == 1, 3 - x, x)
        to_core = jnp.where(f == 1, 1 - c, c)
        for core in range(2):
            group = 2 * z + core
            cut = jnp.where((lane >> 5) == group, lines[k], 0.0)
            cut = jnp.where((lane >> 5) == trc, spread(cut), 0.0)
            cut = cut + pltpu.roll(cut, 15, 0) + pltpu.roll(cut, 14, 0) + pltpu.roll(cut, 13, 0)
            for s in range(4):
                from_column = jnp.where((to_chip == s) & (to_core == core), columns[k], 0.0)
                from_line = jnp.where(holds[k], cut[4 * s : 4 * s + 1], 0.0)
                at = 2 * k + core
                side_ref[s, at : at + 1] = jnp.where(r < 2, from_column, from_line)

    q, r, f = links[2]
    to_chip = jnp.where(f == 1, 3 - x, x)
    ends = jnp.zeros((16, 128), jnp.float32)
    for half in range(2):
        group = jnp.where(f == 1, 3 - (2 * half + c), 2 * half + c)
        piece = jnp.broadcast_to(columns[2 + half], (16, 128))
        piece = spread(jnp.where((lane >> 5) == trc, piece, 0.0))
        ends = jnp.where(((lane >> 5) == group) & (part == to_chip), piece, ends)
    ends_ref[...] = jnp.where(r < 2, ends, jnp.where(holds[2], lines[2], 0.0))


def pack_kernel(own_ref, other_ref, kept_ref, side_ref, ends_ref, after_ref, out_ref):
    _, x, z, c = place_of()
    passed = from_free([other_ref[WROWS * (g // 2) + 8 * (g % 2) : WROWS * (g // 2) + 8 * (g % 2) + 8] for g in range(8)])
    passed = jnp.concatenate([other_ref[WROWS * b + WIN : WROWS * (b + 1)] for b in range(4)] + [passed], 0)
    kept = kept_ref[...]
    ends = ends_ref[...]
    high = iota((16, 128), 1) < FREE
    low = iota((8, 128), 1) < FREE
    end_chip = 3 * z
    next_chip = jnp.where(z == 0, x + 1, x - 1)
    for j in range(4):
        s = (XLEAD + j) % 4
        side = side_ref[s]
        rows = jnp.where((next_chip == s) & (c != z), passed, 0.0)
        rows = jnp.where(end_chip == s, ends, rows)
        rows = jnp.where((x == s) & (c == z), passed, rows)
        for w in range(8):
            window_ref = own_ref if w < 4 else other_ref
            at = WROWS * (w % 4)
            to = WROWS * w
            out_ref[j, to : to + 16] = jnp.where(high, window_ref[at : at + 16], to_free(kept, w))
            out_ref[j, to + 16 : to + 24] = jnp.where(low, window_ref[at + 16 : at + 24], to_free(side, w))
            out_ref[j, to + WIN : to + WROWS] = rows[2 * w : 2 * w + 2]


def halo_sum(slot_ref, skip):
    sides = []
    for w in range(8):
        at = WROWS * w + 16
        sides.append(slot_ref[0, at : at + 8] + slot_ref[1, at : at + 8] + slot_ref[2, at : at + 8] + slot_ref[3, at : at + 8])
    ends = jnp.zeros((16, 128), jnp.float32)
    for s in range(4):
        rows = jnp.concatenate([slot_ref[s, WROWS * w + WIN : WROWS * (w + 1), :] for w in range(8)], 0)
        ends = ends + jnp.where(skip == s, 0.0, rows)
    return jnp.concatenate([from_free(sides), ends], 0)


def deposit(slot_ref, total_ref):
    first_row = 32 * lax.axis_index("tile")
    heads = [
        jnp.concatenate([slot_ref[i // 2, OWN * (i % 2) + e : OWN * (i % 2) + e + 1, :] for i in range(8)], 0)
        for e in range(2)
    ]
    lane = iota((8, 128), 1)
    meta = jnp.where(lane < META + 2, heads[0], pltpu.roll(heads[1], 2, 1))
    corner = meta.astype(jnp.int32)
    r = (corner >> 9) - first_row
    hit = (lane >= META) & (lane < META + 4) & (r > -(WIN + 1)) & (r < 32)
    keys = jnp.where(hit, corner * 32 + 4 * iota((8, 128), 0) + lane - META, -1).astype(jnp.float32)
    total_ref[:, 16:56, :] = jnp.zeros((5, 40, 640), jnp.float32)
    lane = iota((32, 128), 1)
    sub = iota((32, 128), 0)

    def one(carry):
        left, top = carry
        left = jnp.where(left == top, -1.0, left)
        following = jnp.max(left)
        key = top.astype(jnp.int32)
        corner = key >> 5
        i = key & 31
        at = (corner >> 9) - first_row + 24
        b = corner & 511
        off = b & 127
        turn = at & 7
        window = slot_ref[i >> 3, pl.ds(pl.multiple_of((i & 7) * WROWS, 8), WROWS), :]
        window = jnp.concatenate([window, jnp.zeros((8, 128), jnp.float32)], 0)
        window = pltpu.roll(window, turn, 0)
        rows = pl.ds(pl.multiple_of((at >> 3) * 8, 8), 32)
        q = (b >> 7) * 128
        here = pl.ds(pl.multiple_of(q, 128), 128)
        there = pl.ds(pl.multiple_of(q + 128, 128), 128)
        inside = (sub >= turn) & (sub < turn + WIN)
        low_side = inside & (lane >= off) & (lane < off + WIN)
        high_side = inside & (lane < off + WIN - 128)
        for m in range(5):
            moved = pltpu.roll(window, (off - WIN * m + 128) % 128, 1)
            total_ref[m, rows, here] += jnp.where(low_side, moved, 0.0)
            total_ref[m, rows, there] += jnp.where(high_side, moved, 0.0)
        return left, following

    lax.while_loop(lambda carry: carry[1] >= 0.0, one, (keys, jnp.max(keys)))


def deposited(total_ref, m):
    mass = total_ref[m, 24:56, 0:512]
    spill = pltpu.roll(total_ref[m, 16:56, 512:640], 33, 0)[0:32]
    return jnp.concatenate([mass[:, 0:128] + spill, mass[:, 128:512]], 1)


def near_kernel(slot_ref, inner_ref, end_ref, out_ref, halo_ref, total_ref):
    _, x, z, c = place_of()
    halo = halo_sum(slot_ref, lax.rem(x + 4 - XLEAD, 4))
    halo_ref[0:8] = halo[0:8]
    halo_ref[8:24] = halo[8:24] + jnp.where((x == 3 * z) & (c == z), end_ref[...], 0.0)
    deposit(slot_ref, total_ref)
    for m in range(4):
        out_ref[m] = inner_ref[m] + deposited(total_ref, m)
    out_ref[4] = 1.0 + deposited(total_ref, 4)


def final_kernel(slot_ref, near_ref, halo_ref, courant_ref, out_ref, total_ref):
    _, x, z, c = place_of()
    halo = halo_ref[...] + halo_sum(slot_ref, -1)
    chip = lax.rem(x + 4 - XLEAD, 4)
    kept = from_free([slot_ref[chip, WROWS * w : WROWS * w + 16, :] for w in range(8)])
    passed = jnp.concatenate([slot_ref[chip, WROWS * w + WIN : WROWS * (w + 1), :] for w in range(8)], 0)
    crossing = jnp.where(c == z, halo[8:24], passed)
    north = jnp.where(c == 0, crossing, kept)
    south = jnp.where(c == 0, kept, crossing)
    west = jnp.where(c == 0, halo[0:1], halo[1:2])
    east = jnp.where(c == 0, halo[2:3], halo[3:4])
    west = jnp.broadcast_to(west, (128, 128)).T
    east = jnp.broadcast_to(east, (128, 128)).T
    v = courant_ref[1]
    mix = courant_ref[2]
    lane = iota((32, 128), 1)
    first = jnp.where(lane == 0, courant_ref[0, :, 0:128] + mix[:, 0:128], 0.0)
    last = jnp.where(lane == 127, mix[:, 384:512], 0.0)
    line = iota((32, 512), 0)
    above = jnp.where(line == 0, v + mix, 0.0)
    below = jnp.where(line == 31, mix, 0.0)
    for m in range(4):
        value = near_ref[m]
        north_row = jnp.concatenate([north[4 * k + m : 4 * k + m + 1] for k in range(4)], 1)
        south_row = jnp.concatenate([south[4 * k + m : 4 * k + m + 1] for k in range(4)], 1)
        value = value + above * north_row + below * south_row
        left = value[:, 0:128] + first * west[32 * m : 32 * m + 32]
        right = value[:, 384:512] + last * east[32 * m : 32 * m + 32]
        out_ref[m] = jnp.concatenate([left, value[:, 128:384], right], 1)
    deposit(slot_ref, total_ref)
    scale = 1.0 / (near_ref[4] + deposited(total_ref, 4))
    for m in range(4):
        out_ref[m] = (out_ref[m] + deposited(total_ref, m)) * scale


def shape(*dims):
    return jax.ShapeDtypeStruct(dims, jnp.float32)


def dma(n):
    return pltpu.SemaphoreType.DMA((n,))


def cost(bytes_accessed):
    return pl.CostEstimate(flops=bytes_accessed, bytes_accessed=bytes_accessed, transcendentals=0)


def body(parent, courant, edge_links, nest_tracer, nest_weight, nest_map, block_live):
    params = pltpu.CompilerParams(vmem_limit_bytes=32 * 1024 * 1024)
    parent = parent[0, 0]
    courant = courant[0, 0]
    values = nest_tracer[0, :, 0].reshape(4, 4, 32, 128).transpose(0, 2, 1, 3).reshape(4, 128, 128)
    weights = nest_weight[0].reshape(4, 32, 128).transpose(1, 0, 2).reshape(128, 128)
    own, slots, kept = pl.pallas_call(
        pool_kernel,
        out_shape=(shape(OWN, 128), shape(12, 24, 128), shape(16, 128)),
        in_specs=[ANY] * 5,
        out_specs=(VMEM, ANY, VMEM),
        scratch_shapes=[
            pltpu.VMEM((4, 128, 128), jnp.float32),
            pltpu.VMEM((128, 128), jnp.float32),
            pltpu.VMEM((4, 128), jnp.int32),
            pltpu.SMEM((1, 4), jnp.int32),
            pltpu.VMEM((4, 32, 512), jnp.float32),
            pltpu.VMEM((12, 24, 128), jnp.float32),
            dma(6),
        ],
        compiler_params=params,
    )(*[pltpu.with_memory_space_constraint(a, pltpu.HBM) for a in (values, weights, nest_map[0], parent, block_live)])
    other = lax.ppermute(own, "tile", [(t, t ^ 2) for t in range(16)])
    around = [(LEAD + j) % 12 for j in range(12)]
    lines_of_z = [
        [(zz % 6) * 16 + tile_of(x, zz // 6, c) for zz in around] for x in range(4) for c in range(2)
    ]
    slots = lax.all_to_all(slots, ("panel", "tile"), 0, 0, tiled=True, axis_index_groups=lines_of_z)
    side, ends = pl.pallas_call(
        lines_kernel,
        out_shape=(shape(4, 8, 128), shape(16, 128)),
        in_specs=[VMEM, SMEM],
        out_specs=(VMEM, VMEM),
        compiler_params=params,
    )(slots, edge_links)
    inner = pl.pallas_call(
        inner_kernel,
        out_shape=shape(4, 32, 512),
        in_specs=[VMEM, VMEM, ANY],
        out_specs=VMEM,
        compiler_params=params,
        cost_estimate=cost(1 << 20),
    )(parent, courant, own)
    packed = pl.pallas_call(
        pack_kernel,
        out_shape=shape(4, SLOT, 128),
        in_specs=[VMEM, VMEM, VMEM, VMEM, VMEM, ANY],
        out_specs=VMEM,
        compiler_params=params,
    )(own, other, kept, side, ends, inner)
    chips = [[tile_of((XLEAD + j) % 4, z, c) for j in range(4)] for z in range(2) for c in range(2)]
    near = lax.all_to_all(packed, "tile", 0, 0, tiled=True, axis_index_groups=chips)
    far = lax.ppermute(near, "tile", [(t, t ^ 1) for t in range(16)])
    scratch = [pltpu.VMEM((5, 88, 640), jnp.float32)]
    summed, halo = pl.pallas_call(
        near_kernel,
        out_shape=(shape(5, 32, 512), shape(24, 128)),
        in_specs=[VMEM, VMEM, VMEM],
        out_specs=(VMEM, VMEM),
        scratch_shapes=scratch,
        compiler_params=params,
        cost_estimate=cost(1 << 20),
    )(near, inner, ends)
    out = pl.pallas_call(
        final_kernel,
        out_shape=shape(4, 32, 512),
        in_specs=[VMEM, VMEM, VMEM, VMEM],
        out_specs=VMEM,
        scratch_shapes=scratch,
        compiler_params=params,
    )(far, summed, halo, courant)
    return out[None, None]


def solution(mesh):
    placed = (
        P("panel", "lev", None, "tile", None),
        P("panel", "lev", None, "tile", None),
        P(),
        P("panel", "tile", "lev", None, None),
        P("panel", "tile", None),
        P("panel", "tile", None),
        P("panel", "tile"),
    )
    return jax.shard_map(
        body,
        mesh=mesh,
        in_specs=placed,
        out_specs=P("panel", "lev", None, "tile", None),
        check_vma=False,
    )
```

```python
import jax
import jax.numpy as jnp
from jax import lax
from jax.experimental import pallas as pl
from jax.experimental.pallas import tpu as pltpu
from jax.sharding import PartitionSpec as P

WIN = 22
WROWS = 24
FAR = -(64 * 512)
OWN = 4 * WROWS
SLOT = 2 * OWN
META = 110
FREE = 112
LEAD = 10
XLEAD = 2
VMEM = pl.BlockSpec(memory_space=pltpu.VMEM)
SMEM = pl.BlockSpec(memory_space=pltpu.SMEM)
ANY = pl.BlockSpec(memory_space=pl.ANY)


def tile_of(x, z, c):
    return (x * 2 + z) * 2 + c


def place_of():
    t = lax.axis_index("tile")
    return t, t // 4, (t // 2) % 2, t % 2


def lane_rows(line):
    return jnp.concatenate([line[:, 128 * k : 128 * (k + 1)] for k in range(4)], 0)


def three(x):
    hi = x.astype(jnp.bfloat16)
    rest = x - hi.astype(jnp.float32)
    mid = rest.astype(jnp.bfloat16)
    low = (rest - mid.astype(jnp.float32)).astype(jnp.bfloat16)
    return hi, mid, low


def dot(a, b):
    return jnp.dot(a, b, preferred_element_type=jnp.float32)


def dot_exact(a, picks):
    hi, mid, low = three(a)
    return dot(hi, picks) + dot(mid, picks) + dot(low, picks)


def picks_of(mask):
    return mask.astype(jnp.float32).astype(jnp.bfloat16)


def iota(dims, axis):
    return lax.broadcasted_iota(jnp.int32, dims, axis)


def to_free(rows, g):
    return pltpu.roll(rows, (FREE - 16 * g) % 128, 1)


def from_free(parts):
    lane = iota(parts[0].shape, 1) >> 4
    rows = jnp.zeros_like(parts[0])
    for g in range(8):
        rows = jnp.where(lane == g, pltpu.roll(parts[g], (16 * g - FREE + 128) % 128, 1), rows)
    return rows


def pool_kernel(
    x_hbm, w_hbm, map_hbm, parent_hbm, live_hbm, out_ref, slot_hbm, kept_ref,
    x_ref, w_ref, map_ref, live_ref, parent_ref, packet_ref, sems
):
    t, _, _, c = place_of()
    copies = [
        pltpu.make_async_copy(parent_hbm, parent_ref, sems.at[0]),
        pltpu.make_async_copy(live_hbm, live_ref, sems.at[1]),
        pltpu.make_async_copy(map_hbm.at[:, 0:128], map_ref, sems.at[2]),
        pltpu.make_async_copy(w_hbm, w_ref, sems.at[3]),
        pltpu.make_async_copy(x_hbm, x_ref, sems.at[4]),
    ]
    for copy in copies:
        copy.start()
    copies[0].wait()
    first = parent_ref[:, 0, :]
    last = parent_ref[:, 31, :]
    west = parent_ref[:, :, 0:128].reshape(128, 128).T[0:1]
    east = parent_ref[:, :, 384:512].reshape(128, 128).T[127:128]
    line = jnp.where(t == 0, first, last)
    packet = jnp.concatenate([west, east, jnp.zeros((6, 128), jnp.float32), lane_rows(line)], 0)
    for k in range(12):
        packet_ref[k] = packet
    send = pltpu.make_async_copy(packet_ref, slot_hbm, sems.at[5])
    send.start()
    first = lane_rows(first)
    last = lane_rows(last)
    kept_ref[...] = jnp.where(c == 0, last, first)
    edge = jnp.where(c == 0, first, last)
    for copy in copies[1:3]:
        copy.wait()
    row = iota((48, 96), 0)
    col = iota((48, 96), 1)
    odd = (row >= WROWS).astype(jnp.int32)
    nest_row = 2 * (col & 31) + odd
    take = picks_of(((nest_row * 43) >> 7) == row - WROWS * odd)
    row = iota((640, 128), 0)
    col = iota((640, 128), 1)
    gather = picks_of((row >> 7) * WIN + (((row & 63) * 43) >> 7) == col)
    for copy in copies[3:5]:
        copy.wait()
    pieces = []
    for blk in range(4):
        live = live_ref[0, blk].astype(jnp.float32)
        weight = w_ref[pl.ds(blk, 32, stride=4), :] * live
        for m in range(4):
            pieces.append(x_ref[blk, pl.ds(m, 32, stride=4), :] * weight)
        pieces.append(weight)
    parts = jnp.concatenate(three(jnp.concatenate(pieces, 1)), 0)
    halves = dot(take, parts)
    wide = iota((WROWS, halves.shape[1]), 1)
    pooled = jnp.where((wide & 64) == 0, halves[:WROWS], halves[WROWS:])
    pooled = jnp.concatenate([pooled[:, 640 * b : 640 * (b + 1)] for b in range(4)], 0)
    windows = dot_exact(pooled, gather)
    rest = jnp.zeros((8, 128), jnp.float32)
    extra = [e for b in range(4) for e in (to_free(edge[8:16], 2 * b), to_free(edge[8:16], 2 * b + 1), rest)]
    lane = iota((OWN, 128), 1)
    out_ref[...] = jnp.where(lane < FREE, windows, jnp.concatenate(extra, 0))
    lane = iota((1, 128), 1)
    for k in range(2):
        row = out_ref[k : k + 1]
        for e in range(2):
            blk = 2 * k + e
            corner = jnp.where(live_ref[0, blk] != 0, map_ref[blk : blk + 1, 0:1], FAR)
            row = jnp.where(lane == META + e, corner.astype(jnp.float32), row)
        out_ref[k : k + 1] = row
    for b in range(4):
        out_ref[WROWS * b + WIN : WROWS * (b + 1)] = edge[2 * b : 2 * b + 2]
    send.wait()


def inner_kernel(parent_ref, courant_ref, after_ref, out_ref):
    u = courant_ref[0]
    v = courant_ref[1]
    mix = courant_ref[2]
    column = iota((32, 512), 1)
    line = iota((32, 512), 0)
    for m in range(4):
        here = parent_ref[m]
        west = jnp.where(column == 0, 0.0, pltpu.roll(here, 1, 1))
        east = jnp.where(column == 511, 0.0, pltpu.roll(here, 511, 1))
        up = jnp.where(line == 0, 0.0, pltpu.roll(here, 1, 0))
        down = jnp.where(line == 31, 0.0, pltpu.roll(here, 31, 0))
        out_ref[m] = here - u * (here - west) - v * (here - up) + mix * (west + east + up + down - 4.0 * here)


def lines_kernel(slots_ref, links_ref, side_ref, ends_ref):
    _, x, z, c = place_of()
    panel = lax.axis_index("panel")
    sides = (0, 1, 2 + z)
    links = [(links_ref[panel, s, 0], links_ref[panel, s, 1], links_ref[panel, s, 2]) for s in sides]

    def slot_of(q, half):
        return lax.rem(6 * half + q + 12 - LEAD, 12)

    halves = [(0, z ^ links[0][2]), (1, z ^ links[1][2]), (2, 0), (2, 1)]
    columns = []
    for k, half in halves:
        q, r, _ = links[k]
        columns.append(slots_ref[slot_of(q, half), pl.ds(r & 1, 1), :])
    columns = jnp.concatenate(columns + [jnp.zeros((4, 128), jnp.float32)], 0)
    near = iota((128, 128), 0)
    far = iota((128, 128), 1)
    back = dot_exact(columns, picks_of((near ^ 31) == far))
    columns = [jnp.where(links[k][2] == 1, back[i : i + 1], columns[i : i + 1]) for i, (k, _) in enumerate(halves)]
    lines = jnp.concatenate([slots_ref[slot_of(q, r & 1), 8:24, :] for q, r, _ in links], 0)
    back = dot_exact(lines, picks_of((near ^ 127) == far))
    lines = [
        jnp.where(
            links[k][2] == 1,
            jnp.concatenate([back[16 * k + 4 * (3 - p) : 16 * k + 4 * (4 - p)] for p in range(4)], 0),
            lines[16 * k : 16 * (k + 1)],
        )
        for k in range(3)
    ]
    holds = [((r == 2) & (x == 0) & (c == 0)) | ((r == 3) & (x == 3) & (c == 1)) for _, r, _ in links]

    lane = iota((16, 128), 1)
    trc = iota((16, 128), 0) & 3
    part = iota((16, 128), 0) >> 2

    def spread(a):
        return a + pltpu.roll(a, 32, 1) + pltpu.roll(a, 64, 1) + pltpu.roll(a, 96, 1)

    for k in range(2):
        q, r, f = links[k]
        to_chip = jnp.where(f == 1, 3 - x, x)
        to_core = jnp.where(f == 1, 1 - c, c)
        for core in range(2):
            group = 2 * z + core
            cut = jnp.where((lane >> 5) == group, lines[k], 0.0)
            cut = jnp.where((lane >> 5) == trc, spread(cut), 0.0)
            cut = cut + pltpu.roll(cut, 15, 0) + pltpu.roll(cut, 14, 0) + pltpu.roll(cut, 13, 0)
            for s in range(4):
                from_column = jnp.where((to_chip == s) & (to_core == core), columns[k], 0.0)
                from_line = jnp.where(holds[k], cut[4 * s : 4 * s + 1], 0.0)
                at = 2 * k + core
                side_ref[s, at : at + 1] = jnp.where(r < 2, from_column, from_line)

    q, r, f = links[2]
    to_chip = jnp.where(f == 1, 3 - x, x)
    ends = jnp.zeros((16, 128), jnp.float32)
    for half in range(2):
        group = jnp.where(f == 1, 3 - (2 * half + c), 2 * half + c)
        piece = jnp.broadcast_to(columns[2 + half], (16, 128))
        piece = spread(jnp.where((lane >> 5) == trc, piece, 0.0))
        ends = jnp.where(((lane >> 5) == group) & (part == to_chip), piece, ends)
    ends_ref[...] = jnp.where(r < 2, ends, jnp.where(holds[2], lines[2], 0.0))


def pack_kernel(own_ref, other_ref, kept_ref, side_ref, ends_ref, after_ref, out_ref):
    _, x, z, c = place_of()
    passed = from_free([other_ref[WROWS * (g // 2) + 8 * (g % 2) : WROWS * (g // 2) + 8 * (g % 2) + 8] for g in range(8)])
    passed = jnp.concatenate([other_ref[WROWS * b + WIN : WROWS * (b + 1)] for b in range(4)] + [passed], 0)
    kept = kept_ref[...]
    ends = ends_ref[...]
    high = iota((16, 128), 1) < FREE
    low = iota((8, 128), 1) < FREE
    end_chip = 3 * z
    next_chip = jnp.where(z == 0, x + 1, x - 1)
    for j in range(4):
        s = (XLEAD + j) % 4
        side = side_ref[s]
        rows = jnp.where((next_chip == s) & (c != z), passed, 0.0)
        rows = jnp.where(end_chip == s, ends, rows)
        rows = jnp.where((x == s) & (c == z), passed, rows)
        for w in range(8):
            window_ref = own_ref if w < 4 else other_ref
            at = WROWS * (w % 4)
            to = WROWS * w
            out_ref[j, to : to + 16] = jnp.where(high, window_ref[at : at + 16], to_free(kept, w))
            out_ref[j, to + 16 : to + 24] = jnp.where(low, window_ref[at + 16 : at + 24], to_free(side, w))
            out_ref[j, to + WIN : to + WROWS] = rows[2 * w : 2 * w + 2]


def halo_sum(slot_ref, skip):
    sides = []
    for w in range(8):
        at = WROWS * w + 16
        sides.append(slot_ref[0, at : at + 8] + slot_ref[1, at : at + 8] + slot_ref[2, at : at + 8] + slot_ref[3, at : at + 8])
    ends = jnp.zeros((16, 128), jnp.float32)
    for s in range(4):
        rows = jnp.concatenate([slot_ref[s, WROWS * w + WIN : WROWS * (w + 1), :] for w in range(8)], 0)
        ends = ends + jnp.where(skip == s, 0.0, rows)
    return jnp.concatenate([from_free(sides), ends], 0)


def deposit(slot_ref, total_ref):
    first_row = 32 * lax.axis_index("tile")
    heads = [
        jnp.concatenate([slot_ref[i // 2, OWN * (i % 2) + e : OWN * (i % 2) + e + 1, :] for i in range(8)], 0)
        for e in range(2)
    ]
    lane = iota((8, 128), 1)
    meta = jnp.where(lane < META + 2, heads[0], pltpu.roll(heads[1], 2, 1))
    corner = meta.astype(jnp.int32)
    r = (corner >> 9) - first_row
    hit = (lane >= META) & (lane < META + 4) & (r > -(WIN + 1)) & (r < 32)
    keys = jnp.where(hit, corner * 32 + 4 * iota((8, 128), 0) + lane - META, -1).astype(jnp.float32)
    total_ref[:, 16:56, :] = jnp.zeros((5, 40, 640), jnp.float32)
    lane = iota((32, 128), 1)
    sub = iota((32, 128), 0)

    def one(carry):
        left, top = carry
        left = jnp.where(left == top, -1.0, left)
        following = jnp.max(left)
        key = top.astype(jnp.int32)
        corner = key >> 5
        i = key & 31
        at = (corner >> 9) - first_row + 24
        b = corner & 511
        off = b & 127
        turn = at & 7
        window = slot_ref[i >> 3, pl.ds(pl.multiple_of((i & 7) * WROWS, 8), WROWS), :]
        window = jnp.concatenate([window, jnp.zeros((8, 128), jnp.float32)], 0)
        window = pltpu.roll(window, turn, 0)
        rows = pl.ds(pl.multiple_of((at >> 3) * 8, 8), 32)
        q = (b >> 7) * 128
        here = pl.ds(pl.multiple_of(q, 128), 128)
        there = pl.ds(pl.multiple_of(q + 128, 128), 128)
        window = jnp.where((sub >= turn) & (sub < turn + WIN), window, 0.0)
        low_side = (lane >= off) & (lane < off + WIN)
        high_side = lane < off + WIN - 128
        for m in range(5):
            moved = pltpu.roll(window, (off - WIN * m + 128) % 128, 1)
            total_ref[m, rows, here] += jnp.where(low_side, moved, 0.0)

        @pl.when(off > 128 - WIN)
        def _():
            for m in range(5):
                moved = pltpu.roll(window, (off - WIN * m + 128) % 128, 1)
                total_ref[m, rows, there] += jnp.where(high_side, moved, 0.0)

        return left, following

    lax.while_loop(lambda carry: carry[1] >= 0.0, one, (keys, jnp.max(keys)))


def deposited(total_ref, m):
    mass = total_ref[m, 24:56, 0:512]
    spill = pltpu.roll(total_ref[m, 16:56, 512:640], 33, 0)[0:32]
    return jnp.concatenate([mass[:, 0:128] + spill, mass[:, 128:512]], 1)


def near_kernel(slot_ref, inner_ref, end_ref, out_ref, halo_ref, total_ref):
    _, x, z, c = place_of()
    halo = halo_sum(slot_ref, lax.rem(x + 4 - XLEAD, 4))
    halo_ref[0:8] = halo[0:8]
    halo_ref[8:24] = halo[8:24] + jnp.where((x == 3 * z) & (c == z), end_ref[...], 0.0)
    deposit(slot_ref, total_ref)
    for m in range(4):
        out_ref[m] = inner_ref[m] + deposited(total_ref, m)
    out_ref[4] = 1.0 + deposited(total_ref, 4)


def final_kernel(slot_ref, near_ref, halo_ref, courant_ref, out_ref, total_ref):
    _, x, z, c = place_of()
    halo = halo_ref[...] + halo_sum(slot_ref, -1)
    chip = lax.rem(x + 4 - XLEAD, 4)
    kept = from_free([slot_ref[chip, WROWS * w : WROWS * w + 16, :] for w in range(8)])
    passed = jnp.concatenate([slot_ref[chip, WROWS * w + WIN : WROWS * (w + 1), :] for w in range(8)], 0)
    crossing = jnp.where(c == z, halo[8:24], passed)
    north = jnp.where(c == 0, crossing, kept)
    south = jnp.where(c == 0, kept, crossing)
    west = jnp.where(c == 0, halo[0:1], halo[1:2])
    east = jnp.where(c == 0, halo[2:3], halo[3:4])
    west = jnp.broadcast_to(west, (128, 128)).T
    east = jnp.broadcast_to(east, (128, 128)).T
    v = courant_ref[1]
    mix = courant_ref[2]
    lane = iota((32, 128), 1)
    first = jnp.where(lane == 0, courant_ref[0, :, 0:128] + mix[:, 0:128], 0.0)
    last = jnp.where(lane == 127, mix[:, 384:512], 0.0)
    line = iota((32, 512), 0)
    above = jnp.where(line == 0, v + mix, 0.0)
    below = jnp.where(line == 31, mix, 0.0)
    for m in range(4):
        value = near_ref[m]
        north_row = jnp.concatenate([north[4 * k + m : 4 * k + m + 1] for k in range(4)], 1)
        south_row = jnp.concatenate([south[4 * k + m : 4 * k + m + 1] for k in range(4)], 1)
        value = value + above * north_row + below * south_row
        left = value[:, 0:128] + first * west[32 * m : 32 * m + 32]
        right = value[:, 384:512] + last * east[32 * m : 32 * m + 32]
        out_ref[m] = jnp.concatenate([left, value[:, 128:384], right], 1)
    deposit(slot_ref, total_ref)
    scale = 1.0 / (near_ref[4] + deposited(total_ref, 4))
    for m in range(4):
        out_ref[m] = (out_ref[m] + deposited(total_ref, m)) * scale


def shape(*dims):
    return jax.ShapeDtypeStruct(dims, jnp.float32)


def dma(n):
    return pltpu.SemaphoreType.DMA((n,))


def cost(bytes_accessed):
    return pl.CostEstimate(flops=bytes_accessed, bytes_accessed=bytes_accessed, transcendentals=0)


def body(parent, courant, edge_links, nest_tracer, nest_weight, nest_map, block_live):
    params = pltpu.CompilerParams(vmem_limit_bytes=32 * 1024 * 1024)
    parent = parent[0, 0]
    courant = courant[0, 0]
    values = nest_tracer[0, :, 0].reshape(4, 4, 32, 128).transpose(0, 2, 1, 3).reshape(4, 128, 128)
    weights = nest_weight[0].reshape(4, 32, 128).transpose(1, 0, 2).reshape(128, 128)
    own, slots, kept = pl.pallas_call(
        pool_kernel,
        out_shape=(shape(OWN, 128), shape(12, 24, 128), shape(16, 128)),
        in_specs=[ANY] * 5,
        out_specs=(VMEM, ANY, VMEM),
        scratch_shapes=[
            pltpu.VMEM((4, 128, 128), jnp.float32),
            pltpu.VMEM((128, 128), jnp.float32),
            pltpu.VMEM((4, 128), jnp.int32),
            pltpu.SMEM((1, 4), jnp.int32),
            pltpu.VMEM((4, 32, 512), jnp.float32),
            pltpu.VMEM((12, 24, 128), jnp.float32),
            dma(6),
        ],
        compiler_params=params,
    )(*[pltpu.with_memory_space_constraint(a, pltpu.HBM) for a in (values, weights, nest_map[0], parent, block_live)])
    other = lax.ppermute(own, "tile", [(t, t ^ 2) for t in range(16)])
    around = [(LEAD + j) % 12 for j in range(12)]
    lines_of_z = [
        [(zz % 6) * 16 + tile_of(x, zz // 6, c) for zz in around] for x in range(4) for c in range(2)
    ]
    slots = lax.all_to_all(slots, ("panel", "tile"), 0, 0, tiled=True, axis_index_groups=lines_of_z)
    side, ends = pl.pallas_call(
        lines_kernel,
        out_shape=(shape(4, 8, 128), shape(16, 128)),
        in_specs=[VMEM, SMEM],
        out_specs=(VMEM, VMEM),
        compiler_params=params,
    )(slots, edge_links)
    inner = pl.pallas_call(
        inner_kernel,
        out_shape=shape(4, 32, 512),
        in_specs=[VMEM, VMEM, ANY],
        out_specs=VMEM,
        compiler_params=params,
        cost_estimate=cost(1 << 20),
    )(parent, courant, own)
    packed = pl.pallas_call(
        pack_kernel,
        out_shape=shape(4, SLOT, 128),
        in_specs=[VMEM, VMEM, VMEM, VMEM, VMEM, ANY],
        out_specs=VMEM,
        compiler_params=params,
    )(own, other, kept, side, ends, inner)
    chips = [[tile_of((XLEAD + j) % 4, z, c) for j in range(4)] for z in range(2) for c in range(2)]
    near = lax.all_to_all(packed, "tile", 0, 0, tiled=True, axis_index_groups=chips)
    far = lax.ppermute(near, "tile", [(t, t ^ 1) for t in range(16)])
    scratch = [pltpu.VMEM((5, 88, 640), jnp.float32)]
    summed, halo = pl.pallas_call(
        near_kernel,
        out_shape=(shape(5, 32, 512), shape(24, 128)),
        in_specs=[VMEM, VMEM, VMEM],
        out_specs=(VMEM, VMEM),
        scratch_shapes=scratch,
        compiler_params=params,
        cost_estimate=cost(1 << 20),
    )(near, inner, ends)
    out = pl.pallas_call(
        final_kernel,
        out_shape=shape(4, 32, 512),
        in_specs=[VMEM, VMEM, VMEM, VMEM],
        out_specs=VMEM,
        scratch_shapes=scratch,
        compiler_params=params,
    )(far, summed, halo, courant)
    return out[None, None]


def solution(mesh):
    placed = (
        P("panel", "lev", None, "tile", None),
        P("panel", "lev", None, "tile", None),
        P(),
        P("panel", "tile", "lev", None, None),
        P("panel", "tile", None),
        P("panel", "tile", None),
        P("panel", "tile"),
    )
    return jax.shard_map(
        body,
        mesh=mesh,
        in_specs=placed,
        out_specs=P("panel", "lev", None, "tile", None),
        check_vma=False,
    )
```

```python
import jax
import jax.numpy as jnp
from jax import lax
from jax.experimental import pallas as pl
from jax.experimental.pallas import tpu as pltpu
from jax.sharding import PartitionSpec as P

WIN = 22
WROWS = 24
FAR = -(64 * 512)
OWN = 4 * WROWS
SLOT = 2 * OWN
META = 110
FREE = 112
LEAD = 11
XLEAD = 2
VMEM = pl.BlockSpec(memory_space=pltpu.VMEM)
SMEM = pl.BlockSpec(memory_space=pltpu.SMEM)
ANY = pl.BlockSpec(memory_space=pl.ANY)


def tile_of(x, z, c):
    return (x * 2 + z) * 2 + c


def place_of():
    t = lax.axis_index("tile")
    return t, t // 4, (t // 2) % 2, t % 2


def lane_rows(line):
    return jnp.concatenate([line[:, 128 * k : 128 * (k + 1)] for k in range(4)], 0)


def three(x):
    hi = x.astype(jnp.bfloat16)
    rest = x - hi.astype(jnp.float32)
    mid = rest.astype(jnp.bfloat16)
    low = (rest - mid.astype(jnp.float32)).astype(jnp.bfloat16)
    return hi, mid, low


def dot(a, b):
    return jnp.dot(a, b, preferred_element_type=jnp.float32)


def dot_exact(a, picks):
    hi, mid, low = three(a)
    return dot(hi, picks) + dot(mid, picks) + dot(low, picks)


def picks_of(mask):
    return mask.astype(jnp.float32).astype(jnp.bfloat16)


def iota(dims, axis):
    return lax.broadcasted_iota(jnp.int32, dims, axis)


def to_free(rows, g):
    return pltpu.roll(rows, (FREE - 16 * g) % 128, 1)


def from_free(parts):
    lane = iota(parts[0].shape, 1) >> 4
    rows = jnp.zeros_like(parts[0])
    for g in range(8):
        rows = jnp.where(lane == g, pltpu.roll(parts[g], (16 * g - FREE + 128) % 128, 1), rows)
    return rows


def pool_kernel(
    x_hbm, w_hbm, map_hbm, parent_hbm, live_hbm, out_ref, slot_hbm, kept_ref,
    x_ref, w_ref, map_ref, live_ref, parent_ref, packet_ref, sems
):
    t, _, _, c = place_of()
    copies = [
        pltpu.make_async_copy(parent_hbm, parent_ref, sems.at[0]),
        pltpu.make_async_copy(live_hbm, live_ref, sems.at[1]),
        pltpu.make_async_copy(map_hbm.at[:, 0:128], map_ref, sems.at[2]),
        pltpu.make_async_copy(w_hbm, w_ref, sems.at[3]),
        pltpu.make_async_copy(x_hbm, x_ref, sems.at[4]),
    ]
    for copy in copies:
        copy.start()
    copies[0].wait()
    first = parent_ref[:, 0, :]
    last = parent_ref[:, 31, :]
    west = parent_ref[:, :, 0:128].reshape(128, 128).T[0:1]
    east = parent_ref[:, :, 384:512].reshape(128, 128).T[127:128]
    line = jnp.where(t == 0, first, last)
    packet = jnp.concatenate([west, east, jnp.zeros((6, 128), jnp.float32), lane_rows(line)], 0)
    for k in range(12):
        packet_ref[k] = packet
    send = pltpu.make_async_copy(packet_ref, slot_hbm, sems.at[5])
    send.start()
    first = lane_rows(first)
    last = lane_rows(last)
    kept_ref[...] = jnp.where(c == 0, last, first)
    edge = jnp.where(c == 0, first, last)
    for copy in copies[1:3]:
        copy.wait()
    row = iota((48, 96), 0)
    col = iota((48, 96), 1)
    odd = (row >= WROWS).astype(jnp.int32)
    nest_row = 2 * (col & 31) + odd
    take = picks_of(((nest_row * 43) >> 7) == row - WROWS * odd)
    row = iota((640, 128), 0)
    col = iota((640, 128), 1)
    gather = picks_of((row >> 7) * WIN + (((row & 63) * 43) >> 7) == col)
    for copy in copies[3:5]:
        copy.wait()
    pieces = []
    for blk in range(4):
        live = live_ref[0, blk].astype(jnp.float32)
        weight = w_ref[pl.ds(blk, 32, stride=4), :] * live
        for m in range(4):
            pieces.append(x_ref[blk, pl.ds(m, 32, stride=4), :] * weight)
        pieces.append(weight)
    parts = jnp.concatenate(three(jnp.concatenate(pieces, 1)), 0)
    halves = dot(take, parts)
    wide = iota((WROWS, halves.shape[1]), 1)
    pooled = jnp.where((wide & 64) == 0, halves[:WROWS], halves[WROWS:])
    pooled = jnp.concatenate([pooled[:, 640 * b : 640 * (b + 1)] for b in range(4)], 0)
    windows = dot_exact(pooled, gather)
    rest = jnp.zeros((8, 128), jnp.float32)
    extra = [e for b in range(4) for e in (to_free(edge[8:16], 2 * b), to_free(edge[8:16], 2 * b + 1), rest)]
    lane = iota((OWN, 128), 1)
    out_ref[...] = jnp.where(lane < FREE, windows, jnp.concatenate(extra, 0))
    lane = iota((1, 128), 1)
    for k in range(2):
        row = out_ref[k : k + 1]
        for e in range(2):
            blk = 2 * k + e
            corner = jnp.where(live_ref[0, blk] != 0, map_ref[blk : blk + 1, 0:1], FAR)
            row = jnp.where(lane == META + e, corner.astype(jnp.float32), row)
        out_ref[k : k + 1] = row
    for b in range(4):
        out_ref[WROWS * b + WIN : WROWS * (b + 1)] = edge[2 * b : 2 * b + 2]
    send.wait()


def inner_kernel(parent_ref, courant_ref, after_ref, out_ref):
    u = courant_ref[0]
    v = courant_ref[1]
    mix = courant_ref[2]
    column = iota((32, 512), 1)
    line = iota((32, 512), 0)
    for m in range(4):
        here = parent_ref[m]
        west = jnp.where(column == 0, 0.0, pltpu.roll(here, 1, 1))
        east = jnp.where(column == 511, 0.0, pltpu.roll(here, 511, 1))
        up = jnp.where(line == 0, 0.0, pltpu.roll(here, 1, 0))
        down = jnp.where(line == 31, 0.0, pltpu.roll(here, 31, 0))
        out_ref[m] = here - u * (here - west) - v * (here - up) + mix * (west + east + up + down - 4.0 * here)


def lines_kernel(slots_ref, links_ref, side_ref, ends_ref):
    _, x, z, c = place_of()
    panel = lax.axis_index("panel")
    sides = (0, 1, 2 + z)
    links = [(links_ref[panel, s, 0], links_ref[panel, s, 1], links_ref[panel, s, 2]) for s in sides]

    def slot_of(q, half):
        return lax.rem(6 * half + q + 12 - LEAD, 12)

    halves = [(0, z ^ links[0][2]), (1, z ^ links[1][2]), (2, 0), (2, 1)]
    columns = []
    for k, half in halves:
        q, r, _ = links[k]
        columns.append(slots_ref[slot_of(q, half), pl.ds(r & 1, 1), :])
    columns = jnp.concatenate(columns + [jnp.zeros((4, 128), jnp.float32)], 0)
    near = iota((128, 128), 0)
    far = iota((128, 128), 1)
    back = dot_exact(columns, picks_of((near ^ 31) == far))
    columns = [jnp.where(links[k][2] == 1, back[i : i + 1], columns[i : i + 1]) for i, (k, _) in enumerate(halves)]
    lines = jnp.concatenate([slots_ref[slot_of(q, r & 1), 8:24, :] for q, r, _ in links], 0)
    back = dot_exact(lines, picks_of((near ^ 127) == far))
    lines = [
        jnp.where(
            links[k][2] == 1,
            jnp.concatenate([back[16 * k + 4 * (3 - p) : 16 * k + 4 * (4 - p)] for p in range(4)], 0),
            lines[16 * k : 16 * (k + 1)],
        )
        for k in range(3)
    ]
    holds = [((r == 2) & (x == 0) & (c == 0)) | ((r == 3) & (x == 3) & (c == 1)) for _, r, _ in links]

    lane = iota((16, 128), 1)
    trc = iota((16, 128), 0) & 3
    part = iota((16, 128), 0) >> 2

    def spread(a):
        return a + pltpu.roll(a, 32, 1) + pltpu.roll(a, 64, 1) + pltpu.roll(a, 96, 1)

    for k in range(2):
        q, r, f = links[k]
        to_chip = jnp.where(f == 1, 3 - x, x)
        to_core = jnp.where(f == 1, 1 - c, c)
        for core in range(2):
            group = 2 * z + core
            cut = jnp.where((lane >> 5) == group, lines[k], 0.0)
            cut = jnp.where((lane >> 5) == trc, spread(cut), 0.0)
            cut = cut + pltpu.roll(cut, 15, 0) + pltpu.roll(cut, 14, 0) + pltpu.roll(cut, 13, 0)
            for s in range(4):
                from_column = jnp.where((to_chip == s) & (to_core == core), columns[k], 0.0)
                from_line = jnp.where(holds[k], cut[4 * s : 4 * s + 1], 0.0)
                at = 2 * k + core
                side_ref[s, at : at + 1] = jnp.where(r < 2, from_column, from_line)

    q, r, f = links[2]
    to_chip = jnp.where(f == 1, 3 - x, x)
    ends = jnp.zeros((16, 128), jnp.float32)
    for half in range(2):
        group = jnp.where(f == 1, 3 - (2 * half + c), 2 * half + c)
        piece = jnp.broadcast_to(columns[2 + half], (16, 128))
        piece = spread(jnp.where((lane >> 5) == trc, piece, 0.0))
        ends = jnp.where(((lane >> 5) == group) & (part == to_chip), piece, ends)
    ends_ref[...] = jnp.where(r < 2, ends, jnp.where(holds[2], lines[2], 0.0))


def pack_kernel(own_ref, other_ref, kept_ref, side_ref, ends_ref, after_ref, out_ref):
    _, x, z, c = place_of()
    passed = from_free([other_ref[WROWS * (g // 2) + 8 * (g % 2) : WROWS * (g // 2) + 8 * (g % 2) + 8] for g in range(8)])
    passed = jnp.concatenate([other_ref[WROWS * b + WIN : WROWS * (b + 1)] for b in range(4)] + [passed], 0)
    kept = kept_ref[...]
    ends = ends_ref[...]
    high = iota((16, 128), 1) < FREE
    low = iota((8, 128), 1) < FREE
    end_chip = 3 * z
    next_chip = jnp.where(z == 0, x + 1, x - 1)
    for j in range(4):
        s = (XLEAD + j) % 4
        side = side_ref[s]
        rows = jnp.where((next_chip == s) & (c != z), passed, 0.0)
        rows = jnp.where(end_chip == s, ends, rows)
        rows = jnp.where((x == s) & (c == z), passed, rows)
        for w in range(8):
            window_ref = own_ref if w < 4 else other_ref
            at = WROWS * (w % 4)
            to = WROWS * w
            out_ref[j, to : to + 16] = jnp.where(high, window_ref[at : at + 16], to_free(kept, w))
            out_ref[j, to + 16 : to + 24] = jnp.where(low, window_ref[at + 16 : at + 24], to_free(side, w))
            out_ref[j, to + WIN : to + WROWS] = rows[2 * w : 2 * w + 2]


def halo_sum(slot_ref, skip):
    sides = []
    for w in range(8):
        at = WROWS * w + 16
        sides.append(slot_ref[0, at : at + 8] + slot_ref[1, at : at + 8] + slot_ref[2, at : at + 8] + slot_ref[3, at : at + 8])
    ends = jnp.zeros((16, 128), jnp.float32)
    for s in range(4):
        rows = jnp.concatenate([slot_ref[s, WROWS * w + WIN : WROWS * (w + 1), :] for w in range(8)], 0)
        ends = ends + jnp.where(skip == s, 0.0, rows)
    return jnp.concatenate([from_free(sides), ends], 0)


def deposit(slot_ref, total_ref):
    first_row = 32 * lax.axis_index("tile")
    heads = [
        jnp.concatenate([slot_ref[i // 2, OWN * (i % 2) + e : OWN * (i % 2) + e + 1, :] for i in range(8)], 0)
        for e in range(2)
    ]
    lane = iota((8, 128), 1)
    meta = jnp.where(lane < META + 2, heads[0], pltpu.roll(heads[1], 2, 1))
    corner = meta.astype(jnp.int32)
    r = (corner >> 9) - first_row
    hit = (lane >= META) & (lane < META + 4) & (r > -(WIN + 1)) & (r < 32)
    keys = jnp.where(hit, corner * 32 + 4 * iota((8, 128), 0) + lane - META, -1).astype(jnp.float32)
    total_ref[:, 16:56, :] = jnp.zeros((5, 40, 640), jnp.float32)
    lane = iota((32, 128), 1)
    sub = iota((32, 128), 0)

    def one(carry):
        left, top = carry
        left = jnp.where(left == top, -1.0, left)
        following = jnp.max(left)
        key = top.astype(jnp.int32)
        corner = key >> 5
        i = key & 31
        at = (corner >> 9) - first_row + 24
        b = corner & 511
        off = b & 127
        turn = at & 7
        window = slot_ref[i >> 3, pl.ds(pl.multiple_of((i & 7) * WROWS, 8), WROWS), :]
        window = jnp.concatenate([window, jnp.zeros((8, 128), jnp.float32)], 0)
        window = pltpu.roll(window, turn, 0)
        rows = pl.ds(pl.multiple_of((at >> 3) * 8, 8), 32)
        q = (b >> 7) * 128
        here = pl.ds(pl.multiple_of(q, 128), 128)
        there = pl.ds(pl.multiple_of(q + 128, 128), 128)
        window = jnp.where((sub >= turn) & (sub < turn + WIN), window, 0.0)
        low_side = (lane >= off) & (lane < off + WIN)
        high_side = lane < off + WIN - 128
        for m in range(5):
            moved = pltpu.roll(window, (off - WIN * m + 128) % 128, 1)
            total_ref[m, rows, here] += jnp.where(low_side, moved, 0.0)

        @pl.when(off > 128 - WIN)
        def _():
            for m in range(5):
                moved = pltpu.roll(window, (off - WIN * m + 128) % 128, 1)
                total_ref[m, rows, there] += jnp.where(high_side, moved, 0.0)

        return left, following

    lax.while_loop(lambda carry: carry[1] >= 0.0, one, (keys, jnp.max(keys)))


def deposited(total_ref, m):
    mass = total_ref[m, 24:56, 0:512]
    spill = pltpu.roll(total_ref[m, 16:56, 512:640], 33, 0)[0:32]
    return jnp.concatenate([mass[:, 0:128] + spill, mass[:, 128:512]], 1)


def near_kernel(slot_ref, inner_ref, end_ref, out_ref, halo_ref, total_ref):
    _, x, z, c = place_of()
    halo = halo_sum(slot_ref, lax.rem(x + 4 - XLEAD, 4))
    halo_ref[0:8] = halo[0:8]
    halo_ref[8:24] = halo[8:24] + jnp.where((x == 3 * z) & (c == z), end_ref[...], 0.0)
    deposit(slot_ref, total_ref)
    for m in range(4):
        out_ref[m] = inner_ref[m] + deposited(total_ref, m)
    out_ref[4] = 1.0 + deposited(total_ref, 4)


def final_kernel(slot_ref, near_ref, halo_ref, courant_ref, out_ref, total_ref):
    _, x, z, c = place_of()
    halo = halo_ref[...] + halo_sum(slot_ref, -1)
    chip = lax.rem(x + 4 - XLEAD, 4)
    kept = from_free([slot_ref[chip, WROWS * w : WROWS * w + 16, :] for w in range(8)])
    passed = jnp.concatenate([slot_ref[chip, WROWS * w + WIN : WROWS * (w + 1), :] for w in range(8)], 0)
    crossing = jnp.where(c == z, halo[8:24], passed)
    north = jnp.where(c == 0, crossing, kept)
    south = jnp.where(c == 0, kept, crossing)
    west = jnp.where(c == 0, halo[0:1], halo[1:2])
    east = jnp.where(c == 0, halo[2:3], halo[3:4])
    west = jnp.broadcast_to(west, (128, 128)).T
    east = jnp.broadcast_to(east, (128, 128)).T
    v = courant_ref[1]
    mix = courant_ref[2]
    lane = iota((32, 128), 1)
    first = jnp.where(lane == 0, courant_ref[0, :, 0:128] + mix[:, 0:128], 0.0)
    last = jnp.where(lane == 127, mix[:, 384:512], 0.0)
    line = iota((32, 512), 0)
    above = jnp.where(line == 0, v + mix, 0.0)
    below = jnp.where(line == 31, mix, 0.0)
    for m in range(4):
        value = near_ref[m]
        north_row = jnp.concatenate([north[4 * k + m : 4 * k + m + 1] for k in range(4)], 1)
        south_row = jnp.concatenate([south[4 * k + m : 4 * k + m + 1] for k in range(4)], 1)
        value = value + above * north_row + below * south_row
        left = value[:, 0:128] + first * west[32 * m : 32 * m + 32]
        right = value[:, 384:512] + last * east[32 * m : 32 * m + 32]
        out_ref[m] = jnp.concatenate([left, value[:, 128:384], right], 1)
    deposit(slot_ref, total_ref)
    scale = 1.0 / (near_ref[4] + deposited(total_ref, 4))
    for m in range(4):
        out_ref[m] = (out_ref[m] + deposited(total_ref, m)) * scale


def shape(*dims):
    return jax.ShapeDtypeStruct(dims, jnp.float32)


def dma(n):
    return pltpu.SemaphoreType.DMA((n,))


def cost(bytes_accessed):
    return pl.CostEstimate(flops=bytes_accessed, bytes_accessed=bytes_accessed, transcendentals=0)


def body(parent, courant, edge_links, nest_tracer, nest_weight, nest_map, block_live):
    params = pltpu.CompilerParams(vmem_limit_bytes=32 * 1024 * 1024)
    parent = parent[0, 0]
    courant = courant[0, 0]
    values = nest_tracer[0, :, 0].reshape(4, 4, 32, 128).transpose(0, 2, 1, 3).reshape(4, 128, 128)
    weights = nest_weight[0].reshape(4, 32, 128).transpose(1, 0, 2).reshape(128, 128)
    own, slots, kept = pl.pallas_call(
        pool_kernel,
        out_shape=(shape(OWN, 128), shape(12, 24, 128), shape(16, 128)),
        in_specs=[ANY] * 5,
        out_specs=(VMEM, ANY, VMEM),
        scratch_shapes=[
            pltpu.VMEM((4, 128, 128), jnp.float32),
            pltpu.VMEM((128, 128), jnp.float32),
            pltpu.VMEM((4, 128), jnp.int32),
            pltpu.SMEM((1, 4), jnp.int32),
            pltpu.VMEM((4, 32, 512), jnp.float32),
            pltpu.VMEM((12, 24, 128), jnp.float32),
            dma(6),
        ],
        compiler_params=params,
    )(*[pltpu.with_memory_space_constraint(a, pltpu.HBM) for a in (values, weights, nest_map[0], parent, block_live)])
    other = lax.ppermute(own, "tile", [(t, t ^ 2) for t in range(16)])
    around = [(LEAD + j) % 12 for j in range(12)]
    lines_of_z = [
        [(zz % 6) * 16 + tile_of(x, zz // 6, c) for zz in around] for x in range(4) for c in range(2)
    ]
    slots = lax.all_to_all(slots, ("panel", "tile"), 0, 0, tiled=True, axis_index_groups=lines_of_z)
    side, ends = pl.pallas_call(
        lines_kernel,
        out_shape=(shape(4, 8, 128), shape(16, 128)),
        in_specs=[VMEM, SMEM],
        out_specs=(VMEM, VMEM),
        compiler_params=params,
    )(slots, edge_links)
    inner = pl.pallas_call(
        inner_kernel,
        out_shape=shape(4, 32, 512),
        in_specs=[VMEM, VMEM, ANY],
        out_specs=VMEM,
        compiler_params=params,
        cost_estimate=cost(1 << 20),
    )(parent, courant, own)
    packed = pl.pallas_call(
        pack_kernel,
        out_shape=shape(4, SLOT, 128),
        in_specs=[VMEM, VMEM, VMEM, VMEM, VMEM, ANY],
        out_specs=VMEM,
        compiler_params=params,
    )(own, other, kept, side, ends, inner)
    chips = [[tile_of((XLEAD + j) % 4, z, c) for j in range(4)] for z in range(2) for c in range(2)]
    near = lax.all_to_all(packed, "tile", 0, 0, tiled=True, axis_index_groups=chips)
    far = lax.ppermute(near, "tile", [(t, t ^ 1) for t in range(16)])
    scratch = [pltpu.VMEM((5, 88, 640), jnp.float32)]
    summed, halo = pl.pallas_call(
        near_kernel,
        out_shape=(shape(5, 32, 512), shape(24, 128)),
        in_specs=[VMEM, VMEM, VMEM],
        out_specs=(VMEM, VMEM),
        scratch_shapes=scratch,
        compiler_params=params,
        cost_estimate=cost(1 << 20),
    )(near, inner, ends)
    out = pl.pallas_call(
        final_kernel,
        out_shape=shape(4, 32, 512),
        in_specs=[VMEM, VMEM, VMEM, VMEM],
        out_specs=VMEM,
        scratch_shapes=scratch,
        compiler_params=params,
    )(far, summed, halo, courant)
    return out[None, None]


def solution(mesh):
    placed = (
        P("panel", "lev", None, "tile", None),
        P("panel", "lev", None, "tile", None),
        P(),
        P("panel", "tile", "lev", None, None),
        P("panel", "tile", None),
        P("panel", "tile", None),
        P("panel", "tile"),
    )
    return jax.shard_map(
        body,
        mesh=mesh,
        in_specs=placed,
        out_specs=P("panel", "lev", None, "tile", None),
        check_vma=False,
    )
```

```python
import jax
import jax.numpy as jnp
from jax import lax
from jax.experimental import pallas as pl
from jax.experimental.pallas import tpu as pltpu
from jax.sharding import PartitionSpec as P

WIN = 22
WROWS = 24
FAR = -(64 * 512)
OWN = 4 * WROWS
SLOT = 2 * OWN
META = 110
FREE = 112
LEAD = 11
XORD = (2, 1, 3, 0)
VMEM = pl.BlockSpec(memory_space=pltpu.VMEM)
SMEM = pl.BlockSpec(memory_space=pltpu.SMEM)
ANY = pl.BlockSpec(memory_space=pl.ANY)


def tile_of(x, z, c):
    return (x * 2 + z) * 2 + c


def place_of():
    t = lax.axis_index("tile")
    return t, t // 4, (t // 2) % 2, t % 2


def order_of(x):
    at = 0
    for j in range(1, 4):
        at = jnp.where(x == XORD[j], j, at)
    return at


def lane_rows(line):
    return jnp.concatenate([line[:, 128 * k : 128 * (k + 1)] for k in range(4)], 0)


def three(x):
    hi = x.astype(jnp.bfloat16)
    rest = x - hi.astype(jnp.float32)
    mid = rest.astype(jnp.bfloat16)
    low = (rest - mid.astype(jnp.float32)).astype(jnp.bfloat16)
    return hi, mid, low


def dot(a, b):
    return jnp.dot(a, b, preferred_element_type=jnp.float32)


def dot_exact(a, picks):
    hi, mid, low = three(a)
    return dot(hi, picks) + dot(mid, picks) + dot(low, picks)


def picks_of(mask):
    return mask.astype(jnp.float32).astype(jnp.bfloat16)


def iota(dims, axis):
    return lax.broadcasted_iota(jnp.int32, dims, axis)


def to_free(rows, g):
    return pltpu.roll(rows, (FREE - 16 * g) % 128, 1)


def from_free(parts):
    lane = iota(parts[0].shape, 1) >> 4
    rows = jnp.zeros_like(parts[0])
    for g in range(8):
        rows = jnp.where(lane == g, pltpu.roll(parts[g], (16 * g - FREE + 128) % 128, 1), rows)
    return rows


def pool_kernel(
    x_hbm, w_hbm, map_hbm, parent_hbm, live_hbm, out_ref, slot_hbm, kept_ref,
    x_ref, w_ref, map_ref, live_ref, parent_ref, packet_ref, sems
):
    t, _, _, c = place_of()
    copies = [
        pltpu.make_async_copy(parent_hbm, parent_ref, sems.at[0]),
        pltpu.make_async_copy(live_hbm, live_ref, sems.at[1]),
        pltpu.make_async_copy(map_hbm.at[:, 0:128], map_ref, sems.at[2]),
        pltpu.make_async_copy(w_hbm, w_ref, sems.at[3]),
        pltpu.make_async_copy(x_hbm, x_ref, sems.at[4]),
    ]
    for copy in copies:
        copy.start()
    copies[0].wait()
    first = parent_ref[:, 0, :]
    last = parent_ref[:, 31, :]
    west = parent_ref[:, :, 0:128].reshape(128, 128).T[0:1]
    east = parent_ref[:, :, 384:512].reshape(128, 128).T[127:128]
    line = jnp.where(t == 0, first, last)
    packet = jnp.concatenate([west, east, jnp.zeros((6, 128), jnp.float32), lane_rows(line)], 0)
    for k in range(12):
        packet_ref[k] = packet
    send = pltpu.make_async_copy(packet_ref, slot_hbm, sems.at[5])
    send.start()
    first = lane_rows(first)
    last = lane_rows(last)
    kept_ref[...] = jnp.where(c == 0, last, first)
    edge = jnp.where(c == 0, first, last)
    for copy in copies[1:3]:
        copy.wait()
    row = iota((48, 96), 0)
    col = iota((48, 96), 1)
    odd = (row >= WROWS).astype(jnp.int32)
    nest_row = 2 * (col & 31) + odd
    take = picks_of(((nest_row * 43) >> 7) == row - WROWS * odd)
    row = iota((640, 128), 0)
    col = iota((640, 128), 1)
    gather = picks_of((row >> 7) * WIN + (((row & 63) * 43) >> 7) == col)
    for copy in copies[3:5]:
        copy.wait()
    pieces = []
    for blk in range(4):
        live = live_ref[0, blk].astype(jnp.float32)
        weight = w_ref[pl.ds(blk, 32, stride=4), :] * live
        for m in range(4):
            pieces.append(x_ref[blk, pl.ds(m, 32, stride=4), :] * weight)
        pieces.append(weight)
    parts = jnp.concatenate(three(jnp.concatenate(pieces, 1)), 0)
    halves = dot(take, parts)
    wide = iota((WROWS, halves.shape[1]), 1)
    pooled = jnp.where((wide & 64) == 0, halves[:WROWS], halves[WROWS:])
    pooled = jnp.concatenate([pooled[:, 640 * b : 640 * (b + 1)] for b in range(4)], 0)
    windows = dot_exact(pooled, gather)
    rest = jnp.zeros((8, 128), jnp.float32)
    extra = [e for b in range(4) for e in (to_free(edge[8:16], 2 * b), to_free(edge[8:16], 2 * b + 1), rest)]
    lane = iota((OWN, 128), 1)
    out_ref[...] = jnp.where(lane < FREE, windows, jnp.concatenate(extra, 0))
    lane = iota((1, 128), 1)
    for k in range(2):
        row = out_ref[k : k + 1]
        for e in range(2):
            blk = 2 * k + e
            corner = jnp.where(live_ref[0, blk] != 0, map_ref[blk : blk + 1, 0:1], FAR)
            row = jnp.where(lane == META + e, corner.astype(jnp.float32), row)
        out_ref[k : k + 1] = row
    for b in range(4):
        out_ref[WROWS * b + WIN : WROWS * (b + 1)] = edge[2 * b : 2 * b + 2]
    send.wait()


def inner_kernel(parent_ref, courant_ref, after_ref, out_ref):
    u = courant_ref[0]
    v = courant_ref[1]
    mix = courant_ref[2]
    column = iota((32, 512), 1)
    line = iota((32, 512), 0)
    for m in range(4):
        here = parent_ref[m]
        west = jnp.where(column == 0, 0.0, pltpu.roll(here, 1, 1))
        east = jnp.where(column == 511, 0.0, pltpu.roll(here, 511, 1))
        up = jnp.where(line == 0, 0.0, pltpu.roll(here, 1, 0))
        down = jnp.where(line == 31, 0.0, pltpu.roll(here, 31, 0))
        out_ref[m] = here - u * (here - west) - v * (here - up) + mix * (west + east + up + down - 4.0 * here)


def lines_kernel(slots_ref, links_ref, side_ref, ends_ref):
    _, x, z, c = place_of()
    panel = lax.axis_index("panel")
    sides = (0, 1, 2 + z)
    links = [(links_ref[panel, s, 0], links_ref[panel, s, 1], links_ref[panel, s, 2]) for s in sides]

    def slot_of(q, half):
        return lax.rem(6 * half + q + 12 - LEAD, 12)

    halves = [(0, z ^ links[0][2]), (1, z ^ links[1][2]), (2, 0), (2, 1)]
    columns = []
    for k, half in halves:
        q, r, _ = links[k]
        columns.append(slots_ref[slot_of(q, half), pl.ds(r & 1, 1), :])
    columns = jnp.concatenate(columns + [jnp.zeros((4, 128), jnp.float32)], 0)
    near = iota((128, 128), 0)
    far = iota((128, 128), 1)
    back = dot_exact(columns, picks_of((near ^ 31) == far))
    columns = [jnp.where(links[k][2] == 1, back[i : i + 1], columns[i : i + 1]) for i, (k, _) in enumerate(halves)]
    lines = jnp.concatenate([slots_ref[slot_of(q, r & 1), 8:24, :] for q, r, _ in links], 0)
    back = dot_exact(lines, picks_of((near ^ 127) == far))
    lines = [
        jnp.where(
            links[k][2] == 1,
            jnp.concatenate([back[16 * k + 4 * (3 - p) : 16 * k + 4 * (4 - p)] for p in range(4)], 0),
            lines[16 * k : 16 * (k + 1)],
        )
        for k in range(3)
    ]
    holds = [((r == 2) & (x == 0) & (c == 0)) | ((r == 3) & (x == 3) & (c == 1)) for _, r, _ in links]

    lane = iota((16, 128), 1)
    trc = iota((16, 128), 0) & 3
    part = iota((16, 128), 0) >> 2

    def spread(a):
        return a + pltpu.roll(a, 32, 1) + pltpu.roll(a, 64, 1) + pltpu.roll(a, 96, 1)

    for k in range(2):
        q, r, f = links[k]
        to_chip = jnp.where(f == 1, 3 - x, x)
        to_core = jnp.where(f == 1, 1 - c, c)
        for core in range(2):
            group = 2 * z + core
            cut = jnp.where((lane >> 5) == group, lines[k], 0.0)
            cut = jnp.where((lane >> 5) == trc, spread(cut), 0.0)
            cut = cut + pltpu.roll(cut, 15, 0) + pltpu.roll(cut, 14, 0) + pltpu.roll(cut, 13, 0)
            for s in range(4):
                from_column = jnp.where((to_chip == s) & (to_core == core), columns[k], 0.0)
                from_line = jnp.where(holds[k], cut[4 * s : 4 * s + 1], 0.0)
                at = 2 * k + core
                side_ref[s, at : at + 1] = jnp.where(r < 2, from_column, from_line)

    q, r, f = links[2]
    to_chip = jnp.where(f == 1, 3 - x, x)
    ends = jnp.zeros((16, 128), jnp.float32)
    for half in range(2):
        group = jnp.where(f == 1, 3 - (2 * half + c), 2 * half + c)
        piece = jnp.broadcast_to(columns[2 + half], (16, 128))
        piece = spread(jnp.where((lane >> 5) == trc, piece, 0.0))
        ends = jnp.where(((lane >> 5) == group) & (part == to_chip), piece, ends)
    ends_ref[...] = jnp.where(r < 2, ends, jnp.where(holds[2], lines[2], 0.0))


def pack_kernel(own_ref, other_ref, kept_ref, side_ref, ends_ref, after_ref, out_ref):
    _, x, z, c = place_of()
    passed = from_free([other_ref[WROWS * (g // 2) + 8 * (g % 2) : WROWS * (g // 2) + 8 * (g % 2) + 8] for g in range(8)])
    passed = jnp.concatenate([other_ref[WROWS * b + WIN : WROWS * (b + 1)] for b in range(4)] + [passed], 0)
    kept = kept_ref[...]
    ends = ends_ref[...]
    high = iota((16, 128), 1) < FREE
    low = iota((8, 128), 1) < FREE
    end_chip = 3 * z
    next_chip = jnp.where(z == 0, x + 1, x - 1)
    for j in range(4):
        s = XORD[j]
        side = side_ref[s]
        rows = jnp.where((next_chip == s) & (c != z), passed, 0.0)
        rows = jnp.where(end_chip == s, ends, rows)
        rows = jnp.where((x == s) & (c == z), passed, rows)
        for w in range(8):
            window_ref = own_ref if w < 4 else other_ref
            at = WROWS * (w % 4)
            to = WROWS * w
            out_ref[j, to : to + 16] = jnp.where(high, window_ref[at : at + 16], to_free(kept, w))
            out_ref[j, to + 16 : to + 24] = jnp.where(low, window_ref[at + 16 : at + 24], to_free(side, w))
            out_ref[j, to + WIN : to + WROWS] = rows[2 * w : 2 * w + 2]


def halo_sum(slot_ref, skip):
    sides = []
    for w in range(8):
        at = WROWS * w + 16
        sides.append(slot_ref[0, at : at + 8] + slot_ref[1, at : at + 8] + slot_ref[2, at : at + 8] + slot_ref[3, at : at + 8])
    ends = jnp.zeros((16, 128), jnp.float32)
    for s in range(4):
        rows = jnp.concatenate([slot_ref[s, WROWS * w + WIN : WROWS * (w + 1), :] for w in range(8)], 0)
        ends = ends + jnp.where(skip == s, 0.0, rows)
    return jnp.concatenate([from_free(sides), ends], 0)


def deposit(slot_ref, total_ref):
    first_row = 32 * lax.axis_index("tile")
    heads = [
        jnp.concatenate([slot_ref[i // 2, OWN * (i % 2) + e : OWN * (i % 2) + e + 1, :] for i in range(8)], 0)
        for e in range(2)
    ]
    lane = iota((8, 128), 1)
    meta = jnp.where(lane < META + 2, heads[0], pltpu.roll(heads[1], 2, 1))
    corner = meta.astype(jnp.int32)
    r = (corner >> 9) - first_row
    hit = (lane >= META) & (lane < META + 4) & (r > -(WIN + 1)) & (r < 32)
    keys = jnp.where(hit, corner * 32 + 4 * iota((8, 128), 0) + lane - META, -1).astype(jnp.float32)
    total_ref[:, 16:56, :] = jnp.zeros((5, 40, 640), jnp.float32)
    lane = iota((32, 128), 1)
    sub = iota((32, 128), 0)

    def one(carry):
        left, top = carry
        left = jnp.where(left == top, -1.0, left)
        following = jnp.max(left)
        key = top.astype(jnp.int32)
        corner = key >> 5
        i = key & 31
        at = (corner >> 9) - first_row + 24
        b = corner & 511
        off = b & 127
        turn = at & 7
        window = slot_ref[i >> 3, pl.ds(pl.multiple_of((i & 7) * WROWS, 8), WROWS), :]
        window = jnp.concatenate([window, jnp.zeros((8, 128), jnp.float32)], 0)
        window = pltpu.roll(window, turn, 0)
        rows = pl.ds(pl.multiple_of((at >> 3) * 8, 8), 32)
        q = (b >> 7) * 128
        here = pl.ds(pl.multiple_of(q, 128), 128)
        there = pl.ds(pl.multiple_of(q + 128, 128), 128)
        window = jnp.where((sub >= turn) & (sub < turn + WIN), window, 0.0)
        low_side = (lane >= off) & (lane < off + WIN)
        high_side = lane < off + WIN - 128
        for m in range(5):
            moved = pltpu.roll(window, (off - WIN * m + 128) % 128, 1)
            total_ref[m, rows, here] += jnp.where(low_side, moved, 0.0)

        @pl.when(off > 128 - WIN)
        def _():
            for m in range(5):
                moved = pltpu.roll(window, (off - WIN * m + 128) % 128, 1)
                total_ref[m, rows, there] += jnp.where(high_side, moved, 0.0)

        return left, following

    lax.while_loop(lambda carry: carry[1] >= 0.0, one, (keys, jnp.max(keys)))


def deposited(total_ref, m):
    mass = total_ref[m, 24:56, 0:512]
    spill = pltpu.roll(total_ref[m, 16:56, 512:640], 33, 0)[0:32]
    return jnp.concatenate([mass[:, 0:128] + spill, mass[:, 128:512]], 1)


def near_kernel(slot_ref, inner_ref, end_ref, out_ref, halo_ref, total_ref):
    _, x, z, c = place_of()
    halo = halo_sum(slot_ref, order_of(x))
    halo_ref[0:8] = halo[0:8]
    halo_ref[8:24] = halo[8:24] + jnp.where((x == 3 * z) & (c == z), end_ref[...], 0.0)
    deposit(slot_ref, total_ref)
    for m in range(4):
        out_ref[m] = inner_ref[m] + deposited(total_ref, m)
    out_ref[4] = 1.0 + deposited(total_ref, 4)


def final_kernel(slot_ref, near_ref, halo_ref, courant_ref, out_ref, total_ref):
    _, x, z, c = place_of()
    halo = halo_ref[...] + halo_sum(slot_ref, -1)
    chip = order_of(x)
    kept = from_free([slot_ref[chip, WROWS * w : WROWS * w + 16, :] for w in range(8)])
    passed = jnp.concatenate([slot_ref[chip, WROWS * w + WIN : WROWS * (w + 1), :] for w in range(8)], 0)
    crossing = jnp.where(c == z, halo[8:24], passed)
    north = jnp.where(c == 0, crossing, kept)
    south = jnp.where(c == 0, kept, crossing)
    west = jnp.where(c == 0, halo[0:1], halo[1:2])
    east = jnp.where(c == 0, halo[2:3], halo[3:4])
    west = jnp.broadcast_to(west, (128, 128)).T
    east = jnp.broadcast_to(east, (128, 128)).T
    v = courant_ref[1]
    mix = courant_ref[2]
    lane = iota((32, 128), 1)
    first = jnp.where(lane == 0, courant_ref[0, :, 0:128] + mix[:, 0:128], 0.0)
    last = jnp.where(lane == 127, mix[:, 384:512], 0.0)
    line = iota((32, 512), 0)
    above = jnp.where(line == 0, v + mix, 0.0)
    below = jnp.where(line == 31, mix, 0.0)
    for m in range(4):
        value = near_ref[m]
        north_row = jnp.concatenate([north[4 * k + m : 4 * k + m + 1] for k in range(4)], 1)
        south_row = jnp.concatenate([south[4 * k + m : 4 * k + m + 1] for k in range(4)], 1)
        value = value + above * north_row + below * south_row
        left = value[:, 0:128] + first * west[32 * m : 32 * m + 32]
        right = value[:, 384:512] + last * east[32 * m : 32 * m + 32]
        out_ref[m] = jnp.concatenate([left, value[:, 128:384], right], 1)
    deposit(slot_ref, total_ref)
    scale = 1.0 / (near_ref[4] + deposited(total_ref, 4))
    for m in range(4):
        out_ref[m] = (out_ref[m] + deposited(total_ref, m)) * scale


def shape(*dims):
    return jax.ShapeDtypeStruct(dims, jnp.float32)


def dma(n):
    return pltpu.SemaphoreType.DMA((n,))


def cost(bytes_accessed):
    return pl.CostEstimate(flops=bytes_accessed, bytes_accessed=bytes_accessed, transcendentals=0)


def body(parent, courant, edge_links, nest_tracer, nest_weight, nest_map, block_live):
    params = pltpu.CompilerParams(vmem_limit_bytes=32 * 1024 * 1024)
    parent = parent[0, 0]
    courant = courant[0, 0]
    values = nest_tracer[0, :, 0].reshape(4, 4, 32, 128).transpose(0, 2, 1, 3).reshape(4, 128, 128)
    weights = nest_weight[0].reshape(4, 32, 128).transpose(1, 0, 2).reshape(128, 128)
    own, slots, kept = pl.pallas_call(
        pool_kernel,
        out_shape=(shape(OWN, 128), shape(12, 24, 128), shape(16, 128)),
        in_specs=[ANY] * 5,
        out_specs=(VMEM, ANY, VMEM),
        scratch_shapes=[
            pltpu.VMEM((4, 128, 128), jnp.float32),
            pltpu.VMEM((128, 128), jnp.float32),
            pltpu.VMEM((4, 128), jnp.int32),
            pltpu.SMEM((1, 4), jnp.int32),
            pltpu.VMEM((4, 32, 512), jnp.float32),
            pltpu.VMEM((12, 24, 128), jnp.float32),
            dma(6),
        ],
        compiler_params=params,
    )(*[pltpu.with_memory_space_constraint(a, pltpu.HBM) for a in (values, weights, nest_map[0], parent, block_live)])
    other = lax.ppermute(own, "tile", [(t, t ^ 2) for t in range(16)])
    around = [(LEAD + j) % 12 for j in range(12)]
    lines_of_z = [
        [(zz % 6) * 16 + tile_of(x, zz // 6, c) for zz in around] for x in range(4) for c in range(2)
    ]
    slots = lax.all_to_all(slots, ("panel", "tile"), 0, 0, tiled=True, axis_index_groups=lines_of_z)
    side, ends = pl.pallas_call(
        lines_kernel,
        out_shape=(shape(4, 8, 128), shape(16, 128)),
        in_specs=[VMEM, SMEM],
        out_specs=(VMEM, VMEM),
        compiler_params=params,
    )(slots, edge_links)
    inner = pl.pallas_call(
        inner_kernel,
        out_shape=shape(4, 32, 512),
        in_specs=[VMEM, VMEM, ANY],
        out_specs=VMEM,
        compiler_params=params,
        cost_estimate=cost(1 << 20),
    )(parent, courant, own)
    packed = pl.pallas_call(
        pack_kernel,
        out_shape=shape(4, SLOT, 128),
        in_specs=[VMEM, VMEM, VMEM, VMEM, VMEM, ANY],
        out_specs=VMEM,
        compiler_params=params,
    )(own, other, kept, side, ends, inner)
    chips = [[tile_of(XORD[j], z, c) for j in range(4)] for z in range(2) for c in range(2)]
    near = lax.all_to_all(packed, "tile", 0, 0, tiled=True, axis_index_groups=chips)
    far = lax.ppermute(near, "tile", [(t, t ^ 1) for t in range(16)])
    scratch = [pltpu.VMEM((5, 88, 640), jnp.float32)]
    summed, halo = pl.pallas_call(
        near_kernel,
        out_shape=(shape(5, 32, 512), shape(24, 128)),
        in_specs=[VMEM, VMEM, VMEM],
        out_specs=(VMEM, VMEM),
        scratch_shapes=scratch,
        compiler_params=params,
        cost_estimate=cost(1 << 20),
    )(near, inner, ends)
    out = pl.pallas_call(
        final_kernel,
        out_shape=shape(4, 32, 512),
        in_specs=[VMEM, VMEM, VMEM, VMEM],
        out_specs=VMEM,
        scratch_shapes=scratch,
        compiler_params=params,
    )(far, summed, halo, courant)
    return out[None, None]


def solution(mesh):
    placed = (
        P("panel", "lev", None, "tile", None),
        P("panel", "lev", None, "tile", None),
        P(),
        P("panel", "tile", "lev", None, None),
        P("panel", "tile", None),
        P("panel", "tile", None),
        P("panel", "tile"),
    )
    return jax.shard_map(
        body,
        mesh=mesh,
        in_specs=placed,
        out_specs=P("panel", "lev", None, "tile", None),
        check_vma=False,
    )
```
